128 devices in a mesh: tm: 8 (over x, core), chan: 16 (over z, y).
Axes of the slice: x: 4, y: 4, z: 4, core: 2. Of those that a mesh axis runs over, the one named last changes fastest.
Arguments:
- samples: float32 [2, 32768, 2048], P(None, ('tm', 'chan')), may hold values from -6 to 6
- window_taper: float32 [2048], replicated, may hold values from 0.5 to 2
- phase_bins: int32 [32768], P('tm'), may hold values from 0 to 1023
- lag_set: int32 [8], replicated, may hold values from 0 to 1024, as said below
Outputs:
- cyclic_spectrum: float32 [2, 256, 8, 2048], P(None, ('tm', 'chan'))
The draws below stay inside these ranges and needn't reach their ends.
Inputs may be any that keep to these rules, and one draw needn't show every extreme that they name: `lag_set`: 8 distinct lags, the last equal to 1024, the others below it.
All inputs are finite; a program needn't handle non-finite values.
Results may differ from the reference program's by a relative error of at most 0.0076.
Values may be sent and summed in bfloat16 or wider, within the bound.
A program may use at most 128 MiB of HBM per device.

```python
import math
import jax
import jax.numpy as jnp
import numpy as np
from jax import lax

K = 2048
NB = 1024
NH = 256
L = 8
MAXLAG = 1024
FRAMES_TOTAL = 32768


def draw_lag_set(key, part):
    key = jax.random.fold_in(key, 7)
    shuffled = jax.random.permutation(key, MAXLAG)
    return jnp.concatenate([shuffled[:L - 1].astype(jnp.int32), jnp.array([MAXLAG], dtype=jnp.int32)])


def plant(drawn, stream_key, smallest, top_value):
    longest = drawn.shape.index(max(drawn.shape))
    spots = []
    for shift in (0, 1):
        where = [jax.random.randint(jax.random.fold_in(stream_key, axis), (), 0, length) for axis, length in enumerate(drawn.shape)]
        where[longest] = (where[longest] + shift) % drawn.shape[longest]
        spots.append(tuple(where))
    return drawn.at[spots[0]].set(smallest).at[spots[1]].set(top_value)


def steps_of(stream_key, shape, split, least, high):
    loudness, own = 1.0, jax.random.fold_in(stream_key, 6)
    for position, blocks in split:
        draws = jnp.exp(jax.random.uniform(jax.random.fold_in(own, position), (blocks,), jnp.float32, least / len(split), high / len(split)))
        loudness = loudness * jnp.repeat(draws, shape[position] // blocks).reshape([-1 if axis == position else 1 for axis in range(len(shape))])
    return loudness


def rank_bounds(count, lean):
    portions = [(1 << 20) // math.isqrt(grade ** lean) + 1 for grade in range(1, count + 1)]
    width = 1 + sum(portions) // (1 << 30)
    return np.cumsum(np.array([max(1, weight // width) for weight in portions]))


def skewed_ids(rng, shape, amount, skew):
    grid = rank_bounds(amount, skew)
    pick = jax.random.randint(jax.random.fold_in(rng, 1), shape, 0, int(grid[amount - 1]))
    rank = jnp.searchsorted(jnp.asarray(grid, jnp.int32), pick, side="right")
    return jax.random.permutation(jax.random.fold_in(rng, 2), amount)[rank].astype(jnp.int32)


def bell_draw(rng, shape, width, bound, split=(), kind=jnp.bfloat16):
    entries = jax.random.normal(rng, shape, jnp.float32) * width
    if len(split) > 0:
        entries = steps_of(rng, shape, split, -0.22, 0.18) * entries
    return jnp.clip(entries, min=-bound, max=bound).astype(kind)


def setup_inputs(seed: int = 0) -> dict:
    seeds = jax.random.split(jax.random.key(seed), 5)
    return {
        "samples": bell_draw(seeds[0], (2, FRAMES_TOTAL, K), 1.0, 6.0, ((1, 128),), jnp.float32),
        "window_taper": jnp.clip(jnp.exp(jax.random.uniform(seeds[1], (K,), jnp.float32, math.log(0.5), math.log(2.0))), 0.5, 2.0),
        "phase_bins": plant(skewed_ids(seeds[2], (FRAMES_TOTAL,), NB, 2), jax.random.fold_in(seeds[2], 3), 0, NB - 1).astype(jnp.int32),
        "lag_set": draw_lag_set(jax.random.fold_in(seeds[4], 71), 0),
    }


def dft_tables(period, row_index, col_index, factor):
    products = row_index[:, None] * col_index[None, :] % period
    angles = products.astype(jnp.float32) * (2.0 * math.pi / period)
    return (jnp.cos(angles) * factor, jnp.sin(angles) * factor)

def reference(samples, window_taper, phase_bins, lag_set):
    highest = lax.Precision.HIGHEST
    k_index = jnp.arange(K, dtype=jnp.int32)
    chan_cos, chan_sin = dft_tables(K, k_index, k_index, 1.0 / math.sqrt(K))
    chan_cos = chan_cos.astype(jnp.bfloat16).astype(jnp.float32)
    chan_sin = chan_sin.astype(jnp.bfloat16).astype(jnp.float32)
    windowed = (samples * window_taper).astype(jnp.bfloat16)
    win_re = windowed[0].astype(jnp.float32)
    win_im = windowed[1].astype(jnp.float32)
    spec_re = (jnp.dot(win_re, chan_cos, precision=highest) + jnp.dot(win_im, chan_sin, precision=highest)).astype(jnp.bfloat16).astype(jnp.float32)
    spec_im = (jnp.dot(win_im, chan_cos, precision=highest) - jnp.dot(win_re, chan_sin, precision=highest)).astype(jnp.bfloat16).astype(jnp.float32)
    zero_rows = jnp.zeros((MAXLAG, K), jnp.float32)
    padded_re = jnp.concatenate([spec_re, zero_rows], 0)
    padded_im = jnp.concatenate([spec_im, zero_rows], 0)

    def one_lag(lag_value):
        lagged_re = lax.dynamic_slice_in_dim(padded_re, lag_value, FRAMES_TOTAL, 0)
        lagged_im = lax.dynamic_slice_in_dim(padded_im, lag_value, FRAMES_TOTAL, 0)
        prod_re = (spec_re * lagged_re + spec_im * lagged_im).astype(jnp.bfloat16)
        prod_im = (spec_im * lagged_re - spec_re * lagged_im).astype(jnp.bfloat16)
        prod_re = lax.optimization_barrier(prod_re).astype(jnp.float32)
        prod_im = lax.optimization_barrier(prod_im).astype(jnp.float32)
        fold_re = jax.ops.segment_sum(prod_re, phase_bins, NB)
        fold_im = jax.ops.segment_sum(prod_im, phase_bins, NB)
        return (fold_re, fold_im)
    fold_re, fold_im = lax.map(one_lag, lag_set)
    counts = jax.ops.segment_sum(jnp.ones((FRAMES_TOTAL,), jnp.float32), phase_bins, NB)
    inverse = 1.0 / jnp.maximum(counts, 1.0)
    fold_re = fold_re * inverse[None, :, None]
    fold_im = fold_im * inverse[None, :, None]
    harm_index = jnp.arange(1, NH + 1, dtype=jnp.int32)
    bin_index = jnp.arange(NB, dtype=jnp.int32)
    phase_cos, phase_sin = dft_tables(NB, harm_index, bin_index, 1.0 / math.sqrt(NB))
    harm_re = jnp.einsum('hb,lbc->hlc', phase_cos, fold_re, precision=highest) + jnp.einsum('hb,lbc->hlc', phase_sin, fold_im, precision=highest)
    harm_im = jnp.einsum('hb,lbc->hlc', phase_cos, fold_im, precision=highest) - jnp.einsum('hb,lbc->hlc', phase_sin, fold_re, precision=highest)
    freq_index = jnp.arange(L, dtype=jnp.int32)
    lag_cos, lag_sin = dft_tables(2 * MAXLAG, freq_index, lag_set.astype(jnp.int32), 1.0 / math.sqrt(L))
    out_re = jnp.einsum('ql,hlc->hqc', lag_cos, harm_re, precision=highest) + jnp.einsum('ql,hlc->hqc', lag_sin, harm_im, precision=highest)
    out_im = jnp.einsum('ql,hlc->hqc', lag_cos, harm_im, precision=highest) - jnp.einsum('ql,hlc->hqc', lag_sin, harm_re, precision=highest)
    return jnp.stack([out_re, out_im], 0)
```

```python
import math

import jax
import jax.numpy as jnp
import ml_dtypes
import numpy as np
from jax import lax
from jax.experimental import pallas as pl
from jax.experimental.pallas import tpu as pltpu
from jax.sharding import PartitionSpec as P

K = 2048
NB = 1024
NH = 256
L = 8
MAXLAG = 1024
T = 32768
NDEV = 128
FR = T // NDEV
CH = K // NDEV
RADIX = 4
KR = K // RADIX
BLK = T // 128
PADBLK = 16
CHUNK = 8
STEPS = BLK // CHUNK
F32 = jnp.float32
BF16 = jnp.bfloat16
NT = (((1,), (1,)), ((), ()))
VMEM = pl.BlockSpec(memory_space=pltpu.VMEM)
SMEM = pl.BlockSpec(memory_space=pltpu.SMEM)
ANY = pl.BlockSpec(memory_space=pl.ANY)


def chan_tables():
    r = np.arange(RADIX)[:, None, None]
    i = np.arange(NDEV // RADIX)[None, :, None]
    j = np.arange(CH)[None, None, :]
    chan = (NDEV * j + RADIX * i + r).reshape(-1)
    angle = (chan[:, None] * np.arange(KR)[None, :] % K) * (2.0 * math.pi / K)
    both = np.concatenate([np.cos(angle), np.sin(angle)], 1).astype(np.float32) * np.float32(1.0 / math.sqrt(K))
    return both.astype(ml_dtypes.bfloat16).reshape(RADIX, K // RADIX, 2 * KR)


def dft_kernel(samples, taper, table, spec, held, tab, ya, yb, sem_s, sem_t):
    parts = 4
    rows = FR // parts
    loads = []
    for p in range(parts):
        part = pl.ds(p * rows, rows)
        loads.append(pltpu.make_async_copy(samples.at[:, part], held.at[:, part], sem_s.at[p]))
        loads[-1].start()
    tables = []
    for r in range(RADIX):
        tables.append(pltpu.make_async_copy(table.at[r], tab.at[r], sem_t.at[r]))
        tables[-1].start()

    for p in range(parts):
        loads[p].wait()

        @pl.loop(0, rows // 16)
        def _(g):
            at = pl.ds(pl.multiple_of(p * rows + g * 16, 16), 16)
            for b in range(KR // 128):
                x = []
                for m in range(RADIX):
                    lanes = pl.ds(m * KR + b * 128, 128)
                    w = taper[:, lanes]
                    x.append([(held[c, at, lanes] * w).astype(BF16).astype(F32) for c in range(2)])
                er, ei = x[0][0] + x[2][0], x[0][1] + x[2][1]
                fr, fi = x[1][0] + x[3][0], x[1][1] + x[3][1]
                gr, gi = x[0][0] - x[2][0], x[0][1] - x[2][1]
                hr, hi = x[1][0] - x[3][0], x[1][1] - x[3][1]
                y = [(er + fr, ei + fi), (gr + hi, gi - hr), (er - fr, ei - fi), (gr - hi, gi + hr)]
                for r in range(RADIX):
                    re, im = y[r][0].astype(BF16), y[r][1].astype(BF16)
                    ya[r, at, pl.ds(b * 128, 128)] = re
                    ya[r, at, pl.ds(KR + b * 128, 128)] = im
                    yb[r, at, pl.ds(b * 128, 128)] = im
                    yb[r, at, pl.ds(KR + b * 128, 128)] = -re

    for r in range(RADIX):
        tables[r].wait()
        re = lax.dot_general(tab[r], ya[r], NT, preferred_element_type=F32)
        spec[:, r, 0:CH, :] = re.astype(BF16).reshape(NDEV // RADIX, CH, FR)
        im = lax.dot_general(tab[r], yb[r], NT, preferred_element_type=F32)
        spec[:, r, CH : 2 * CH, :] = im.astype(BF16).reshape(NDEV // RADIX, CH, FR)


def channelize(samples, window_taper, table):
    return pl.pallas_call(
        dft_kernel,
        out_shape=jax.ShapeDtypeStruct((NDEV // RADIX, RADIX, 2 * CH, FR), BF16),
        in_specs=[ANY, VMEM, ANY],
        out_specs=VMEM,
        scratch_shapes=[
            pltpu.VMEM((2, FR, K), F32),
            pltpu.VMEM((RADIX, K // RADIX, 2 * KR), BF16),
            pltpu.VMEM((RADIX, FR, 2 * KR), BF16),
            pltpu.VMEM((RADIX, FR, 2 * KR), BF16),
            pltpu.SemaphoreType.DMA((4,)),
            pltpu.SemaphoreType.DMA((RADIX,)),
        ],
        compiler_params=pltpu.CompilerParams(vmem_limit_bytes=40 * 2**20),
        name="channelize",
    )(samples, window_taper.reshape(1, K), table)


def sincos(m):
    x = (m - 512).astype(F32) * (math.pi / NB)
    z = x * x
    s = x * (1.0 + z * (-1.0 / 6 + z * (1.0 / 120 + z * (-1.0 / 5040 + z * (1.0 / 362880 - z / 39916800)))))
    c = 1.0 + z * (-0.5 + z * (1.0 / 24 + z * (-1.0 / 720 + z * (1.0 / 40320 + z * (-1.0 / 3628800 + z / 479001600)))))
    return 2.0 * s * s - 1.0, -2.0 * s * c


def rotated(e, f):
    return e[0] * f[0] - e[1] * f[1], e[0] * f[1] + e[1] * f[0]


def table_kernel(bins, table, high, low, weight):
    row32 = lax.broadcasted_iota(jnp.int32, (32, 128), 0)

    @pl.loop(0, BLK)
    def _(m):
        b = bins[pl.ds(m, 1), :]
        lanes = pl.ds(pl.multiple_of(m * 128, 128), 128)
        high[:, lanes] = ((b >> 5) == row32).astype(F32).astype(BF16)
        low[:, lanes] = ((b & 31) == row32).astype(F32).astype(BF16)

    part = 4096
    hist = jnp.zeros((32, 32), F32)
    for p in range(T // part):
        lanes = pl.ds(p * part, part)
        hist = hist + lax.dot_general(high[:, lanes], low[:, lanes], NT, preferred_element_type=F32)
    inverse = (1.0 / math.sqrt(NB)) / jnp.maximum(hist, 1.0)
    first = inverse.astype(BF16)
    second = (inverse - first.astype(F32)).astype(BF16)

    @pl.loop(0, T // part)
    def _(p):
        lanes = pl.ds(pl.multiple_of(p * part, part), part)
        rows = jnp.dot(first, low[:, lanes], preferred_element_type=F32) + jnp.dot(
            second, low[:, lanes], preferred_element_type=F32
        )
        weight[:, lanes] = jnp.sum(rows * high[:, lanes].astype(F32), axis=0, keepdims=True)

    odd = 2 * lax.broadcasted_iota(jnp.int32, (8, 128), 0) + 1

    @pl.loop(0, BLK)
    def _(m):
        b = bins[pl.ds(m, 1), :]
        lanes = pl.ds(pl.multiple_of(m * 128, 128), 128)
        w = weight[:, lanes]
        c, s = sincos((odd * b) & (NB - 1))
        one = (c[0:1], s[0:1])
        even = rotated((c, s), one)
        turn = (even[0][7:8], even[1][7:8])
        twice = 2.0 * turn[0]
        for parity, start in ((0, (c, s)), (1, even)):
            before = (start[0] * w, start[1] * w)
            now = rotated(before, turn)
            for g in range(8):
                for k in range(2):
                    rows = pl.ds(k * NH + parity * 128 + g * 16, 16)
                    table[rows, lanes] = jnp.concatenate([before[k], now[k]], 0).astype(BF16)
                if g < 7:
                    after = (twice * now[0] - before[0], twice * now[1] - before[1])
                    later = (twice * after[0] - now[0], twice * after[1] - now[1])
                    before, now = after, later


def phase_table(bins):
    return pl.pallas_call(
        table_kernel,
        out_shape=jax.ShapeDtypeStruct((2 * NH, T), BF16),
        in_specs=[VMEM],
        out_specs=VMEM,
        scratch_shapes=[
            pltpu.VMEM((32, T), BF16),
            pltpu.VMEM((32, T), BF16),
            pltpu.VMEM((1, T), F32),
        ],
        compiler_params=pltpu.CompilerParams(vmem_limit_bytes=56 * 2**20),
        name="phase_table",
    )(bins)


def fold_kernel(lags, spec, mix_c, mix_s, table, out, xs, prod, acc):
    step = pl.program_id(0)

    @pl.when(step == 0)
    def _():
        acc[...] = jnp.zeros_like(acc)
        xs[pl.ds(BLK, PADBLK)] = jnp.zeros((PADBLK, 2 * CH, 128), BF16)

        @pl.loop(0, NDEV)
        def _(s):
            xs[2 * s] = spec[s, :, 0:128]
            xs[2 * s + 1] = spec[s, :, 128:256]

    lane = lax.broadcasted_iota(jnp.int32, (CH, 128), 1)
    first = step * CHUNK
    for l in range(L):
        lag = lags[l]
        whole, rest = lag >> 7, lag & 127
        back = (128 - rest) & 127
        inside = lane < 128 - rest
        moved = None
        for b in range(CHUNK + 1):
            there = xs[first + b + whole]
            ahead = [
                pltpu.roll(there[k * CH : (k + 1) * CH], back, 1).astype(F32) for k in range(2)
            ]
            if b > 0:
                here = xs[first + b - 1].astype(F32)
                re, im = here[0:CH], here[CH : 2 * CH]
                lre = jnp.where(inside, moved[0], ahead[0])
                lim = jnp.where(inside, moved[1], ahead[1])
                lanes = pl.ds((b - 1) * 128, 128)
                prod[pl.ds(l * 2 * CH, CH), lanes] = (re * lre + im * lim).astype(BF16)
                prod[pl.ds(l * 2 * CH + CH, CH), lanes] = (im * lre - re * lim).astype(BF16)
            moved = ahead

    acc[...] += lax.dot_general(table[...], prod[...], NT, preferred_element_type=F32)

    @pl.when(step == STEPS - 1)
    def _():
        res = jnp.dot(
            acc[0:NH], mix_c[...], preferred_element_type=F32, precision=lax.Precision.HIGHEST
        ) + jnp.dot(
            acc[NH:], mix_s[...], preferred_element_type=F32, precision=lax.Precision.HIGHEST
        )
        out[:, 0:256] = res[0:128]
        out[:, 256:512] = res[128:256]


def fold(lags, spec, mix_c, mix_s, table):
    return pl.pallas_call(
        fold_kernel,
        grid=(STEPS,),
        out_shape=jax.ShapeDtypeStruct((NDEV, 2 * L * 2 * CH), F32),
        in_specs=[SMEM, VMEM, VMEM, VMEM, pl.BlockSpec((2 * NH, CHUNK * 128), lambda i: (0, i))],
        out_specs=pl.BlockSpec((NDEV, 2 * L * 2 * CH), lambda i: (0, 0)),
        scratch_shapes=[
            pltpu.VMEM((BLK + PADBLK, 2 * CH, 128), BF16),
            pltpu.VMEM((L * 2 * CH, CHUNK * 128), BF16),
            pltpu.VMEM((2 * NH, L * 2 * CH), F32),
        ],
        compiler_params=pltpu.CompilerParams(vmem_limit_bytes=32 * 2**20),
        name="fold",
    )(lags, spec, mix_c, mix_s, table)


def place_kernel(got, out):
    turned = got[...].T
    for p in range(2):
        for j in range(CH):
            for ro in range(2):
                row = p * 256 + j * 16 + ro * 8
                out[ro, p, :, j * 128 : (j + 1) * 128] = turned[row : row + 8]


def place(got):
    return pl.pallas_call(
        place_kernel,
        out_shape=jax.ShapeDtypeStruct((2, 2, L, K), F32),
        in_specs=[VMEM],
        out_specs=VMEM,
        name="place",
    )(got)


def lag_mix(lag_set):
    q = jnp.arange(L, dtype=jnp.int32)
    angle = ((lag_set[:, None] * q[None, :]) % (2 * MAXLAG)).astype(F32) * (math.pi / MAXLAG)
    c = jnp.cos(angle) * (1.0 / math.sqrt(L))
    s = jnp.sin(angle) * (1.0 / math.sqrt(L))
    of_cos = jnp.stack([jnp.stack([c, -s], 1), jnp.stack([s, c], 1)], 1)
    of_sin = jnp.stack([jnp.stack([-s, -c], 1), jnp.stack([c, -s], 1)], 1)
    eye = jnp.eye(CH, dtype=F32)

    def spread(m):
        return (m[:, :, None, None] * eye[None, None, :, :, None, None]).reshape(L * 2 * CH, CH * 2 * L)

    return spread(of_cos), spread(of_sin)


def on_device(samples, window_taper, phase_bins, lag_set):
    bins = lax.all_gather(phase_bins.reshape(-1, 128), "tm", tiled=True)
    spec = channelize(samples, window_taper, jnp.asarray(chan_tables()))
    spec = spec.reshape(NDEV, 2 * CH, FR)
    got = lax.all_to_all(spec, ("tm", "chan"), split_axis=0, concat_axis=0, tiled=True)
    table = phase_table(bins)
    mix_c, mix_s = lag_mix(lag_set)
    mine = fold(lag_set, got, mix_c, mix_s, table)
    back = lax.all_to_all(mine, ("tm", "chan"), split_axis=0, concat_axis=0, tiled=True)
    return place(back)


def solution(mesh):
    placed = (P(None, ("tm", "chan"), None), P(), P("tm"), P())
    return jax.shard_map(
        on_device,
        mesh=mesh,
        in_specs=placed,
        out_specs=P(None, ("tm", "chan"), None, None),
        check_vma=False,
    )
```

```python
import math

import jax
import jax.numpy as jnp
import ml_dtypes
import numpy as np
from jax import lax
from jax.experimental import pallas as pl
from jax.experimental.pallas import tpu as pltpu
from jax.sharding import PartitionSpec as P

K = 2048
NB = 1024
NH = 256
L = 8
MAXLAG = 1024
T = 32768
NDEV = 128
FR = T // NDEV
CH = K // NDEV
RADIX = 4
KR = K // RADIX
GROUP = NDEV // RADIX
BLK = T // 128
PADBLK = 32
CHUNK = 8
STEPS = BLK // CHUNK
PARTS = 4
WIDE = 4
F32 = jnp.float32
BF16 = jnp.bfloat16
NT = (((1,), (1,)), ((), ()))
VMEM = pl.BlockSpec(memory_space=pltpu.VMEM)
SMEM = pl.BlockSpec(memory_space=pltpu.SMEM)
ANY = pl.BlockSpec(memory_space=pl.ANY)
MESH = pl.DeviceIdType.MESH


def chan_tables():
    r = np.arange(RADIX)[:, None, None]
    i = np.arange(GROUP)[None, :, None]
    j = np.arange(CH)[None, None, :]
    chan = (NDEV * j + RADIX * i + r).reshape(-1)
    angle = (chan[:, None] * np.arange(KR)[None, :] % K) * (2.0 * math.pi / K)
    both = np.concatenate([np.cos(angle), np.sin(angle)], 1).astype(np.float32) * np.float32(1.0 / math.sqrt(K))
    return both.astype(ml_dtypes.bfloat16).reshape(RADIX, K // RADIX, 2 * KR)


def butterflies(held, taper, ya, yb, part):
    rows = FR // PARTS

    @pl.loop(0, rows // 16)
    def _(g):
        at = pl.ds(pl.multiple_of(part * rows + g * 16, 16), 16)
        for b in range(KR // 128):
            x = []
            for m in range(RADIX):
                lanes = pl.ds(m * KR + b * 128, 128)
                w = taper[:, lanes]
                x.append([(held[c, at, lanes] * w).astype(BF16).astype(F32) for c in range(2)])
            er, ei = x[0][0] + x[2][0], x[0][1] + x[2][1]
            fr, fi = x[1][0] + x[3][0], x[1][1] + x[3][1]
            gr, gi = x[0][0] - x[2][0], x[0][1] - x[2][1]
            hr, hi = x[1][0] - x[3][0], x[1][1] - x[3][1]
            y = [(er + fr, ei + fi), (gr + hi, gi - hr), (er - fr, ei - fi), (gr - hi, gi + hr)]
            for r in range(RADIX):
                re, im = y[r][0].astype(BF16), y[r][1].astype(BF16)
                ya[r, at, pl.ds(b * 128, 128)] = re
                ya[r, at, pl.ds(KR + b * 128, 128)] = im
                yb[r, at, pl.ds(b * 128, 128)] = im
                yb[r, at, pl.ds(KR + b * 128, 128)] = -re


def sincos(m, period):
    x = (m - period // 2).astype(F32) * (math.pi / period)
    z = x * x
    s = x * (1.0 + z * (-1.0 / 6 + z * (1.0 / 120 + z * (-1.0 / 5040 + z * (1.0 / 362880 - z / 39916800)))))
    c = 1.0 + z * (-0.5 + z * (1.0 / 24 + z * (-1.0 / 720 + z * (1.0 / 40320 + z * (-1.0 / 3628800 + z / 479001600)))))
    return 2.0 * s * s - 1.0, -2.0 * s * c


def rotated(e, f):
    return e[0] * f[0] - e[1] * f[1], e[0] * f[1] + e[1] * f[0]


def bins_of(bins, first):
    return jnp.concatenate([bins[pl.ds(first + i, 1), :] for i in range(WIDE)], 1)


def frame_weights(bins, high, low, weight):
    span = WIDE * 128
    row32 = lax.broadcasted_iota(jnp.int32, (32, span), 0)

    @pl.loop(0, BLK // WIDE)
    def _(m):
        b = bins_of(bins, m * WIDE)
        lanes = pl.ds(pl.multiple_of(m * span, span), span)
        high[:, lanes] = ((b >> 5) == row32).astype(F32).astype(BF16)
        low[:, lanes] = ((b & 31) == row32).astype(F32).astype(BF16)

    part = 4096
    hist = jnp.zeros((32, 32), F32)
    for p in range(T // part):
        lanes = pl.ds(p * part, part)
        hist = hist + lax.dot_general(high[:, lanes], low[:, lanes], NT, preferred_element_type=F32)
    inverse = (1.0 / math.sqrt(NB)) / jnp.maximum(hist, 1.0)
    first = inverse.astype(BF16)
    second = (inverse - first.astype(F32)).astype(BF16)

    @pl.loop(0, T // 1024)
    def _(p):
        lanes = pl.ds(pl.multiple_of(p * 1024, 1024), 1024)
        rows = jnp.dot(first, low[:, lanes], preferred_element_type=F32) + jnp.dot(
            second, low[:, lanes], preferred_element_type=F32
        )
        weight[:, lanes] = jnp.sum(rows * high[:, lanes].astype(F32), axis=0, keepdims=True)


def fill_table(bins, weight, table):
    span = WIDE * 128
    odd = 2 * lax.broadcasted_iota(jnp.int32, (8, span), 0) + 1

    @pl.loop(0, BLK // WIDE)
    def _(m):
        b = bins_of(bins, m * WIDE)
        lanes = pl.ds(pl.multiple_of(m * span, span), span)
        w = weight[:, lanes]
        c, s = sincos((odd * b) & (NB - 1), NB)
        one = (c[0:1], s[0:1])
        even = rotated((c, s), one)
        turn = (even[0][7:8], even[1][7:8])
        twice = 2.0 * turn[0]
        for parity, start in ((0, (c, s)), (1, even)):
            before = (start[0] * w, start[1] * w)
            now = rotated(before, turn)
            for g in range(8):
                for k in range(2):
                    rows = pl.ds(k * NH + parity * 128 + g * 16, 16)
                    table[rows, lanes] = jnp.concatenate([before[k], now[k]], 0).astype(BF16)
                if g < 7:
                    after = (twice * now[0] - before[0], twice * now[1] - before[1])
                    later = (twice * after[0] - now[0], twice * after[1] - now[1])
                    before, now = after, later


def fill_mix(lags, mix):
    shape = (2 * CH, CH * 2 * L)
    row = lax.broadcasted_iota(jnp.int32, shape, 0)
    col = lax.broadcasted_iota(jnp.int32, shape, 1)
    part_in, chan_in = row >> 4, row & 15
    chan_out, part_out, q = col >> 4, (col >> 3) & 1, col & 7
    here = jnp.where(chan_in == chan_out, 1.0 / math.sqrt(L), 0.0)
    same = part_in == part_out
    sign = jnp.where(part_in == 0, -1.0, 1.0)
    for l in range(L):
        c, s = sincos((lags[l] * q) & (2 * MAXLAG - 1), 2 * MAXLAG)
        rows = pl.ds(l * 2 * CH, 2 * CH)
        mix[0, rows, :] = here * jnp.where(same, c, sign * s)
        mix[1, rows, :] = here * jnp.where(same, -s, sign * c)


def spread_spectra(got, xs):
    xs[pl.ds(BLK, PADBLK)] = jnp.zeros((PADBLK, 2 * CH, 128), BF16)

    @pl.loop(0, NDEV // 8)
    def _(g):
        for e in range(8):
            s = g * 8 + e
            xs[2 * s] = got[s, :, 0:128]
            xs[2 * s + 1] = got[s, :, 128:256]


def fold(lags, xs, table, prod_a, prod_b, acc):
    lane = lax.broadcasted_iota(jnp.int32, (CH, 128), 1)

    def products(step, prod):
        first = step * CHUNK
        for l in range(L):
            lag = lags[l]
            whole, rest = lag >> 7, lag & 127
            back = (128 - rest) & 127
            inside = lane < 128 - rest
            moved = None
            for b in range(CHUNK + 1):
                there = xs[first + b + whole]
                ahead = [pltpu.roll(there[k * CH : (k + 1) * CH], back, 1).astype(F32) for k in range(2)]
                if b > 0:
                    here = xs[first + b - 1].astype(F32)
                    re, im = here[0:CH], here[CH : 2 * CH]
                    lre = jnp.where(inside, moved[0], ahead[0])
                    lim = jnp.where(inside, moved[1], ahead[1])
                    lanes = pl.ds((b - 1) * 128, 128)
                    prod[pl.ds(l * 2 * CH, CH), lanes] = (re * lre + im * lim).astype(BF16)
                    prod[pl.ds(l * 2 * CH + CH, CH), lanes] = (im * lre - re * lim).astype(BF16)
                moved = ahead

    def add(step, prod):
        lanes = pl.ds(pl.multiple_of(step * CHUNK * 128, CHUNK * 128), CHUNK * 128)
        acc[...] += lax.dot_general(prod[...], table[:, lanes], NT, preferred_element_type=F32)

    acc[...] = jnp.zeros_like(acc)
    products(0, prod_a)

    @pl.loop(0, STEPS // 2)
    def _(i):
        add(2 * i, prod_a)
        products(2 * i + 1, prod_b)
        add(2 * i + 1, prod_b)
        products(2 * i + 2, prod_a)


def kernel(
    lags, samples, taper, chans, own_bins, out,
    held, tab, ya, yb, spec, got, bins, weight, xs, table, prod_a, prod_b, acc, mix, mine, theirs,
    sem_s, sem_t, bin_send, bin_recv, spec_send, spec_recv, last_send, last_recv,
):
    tm, ch = lax.axis_index("tm"), lax.axis_index("chan")
    me = tm * 16 + ch
    x, core, z, y = tm // 2, tm % 2, ch // 4, ch % 4

    def partner(dx, dc, dz, dy):
        return ((x + dx) % 4) * 2 + (core + dc) % 2, ((z + dz) % 4) * 4 + (y + dy) % 4

    barrier = pltpu.get_barrier_semaphore()

    rows = FR // PARTS
    loads = []
    for p in range(PARTS):
        part = pl.ds(p * rows, rows)
        loads.append(pltpu.make_async_copy(samples.at[:, part], held.at[:, part], sem_s.at[p]))
        loads[-1].start()
    tables = []
    for r in range(RADIX):
        tables.append(pltpu.make_async_copy(chans.at[r], tab.at[r], sem_t.at[r]))
        tables[-1].start()

    @pl.loop(1, NDEV)
    def _(i):
        to = (me + i) % NDEV
        pl.semaphore_signal(barrier, inc=1, device_id=(to // 16, to % 16), device_id_type=MESH)

    for p in range(PARTS):
        loads[p].wait()
        butterflies(held, taper, ya, yb, p)

    pl.semaphore_wait(barrier, NDEV - 1)

    bins[pl.ds(pl.multiple_of(tm * 32, 32), 32), :] = own_bins[...]

    @pl.loop(1, 8)
    def _(i):
        pltpu.make_async_remote_copy(
            src_ref=own_bins,
            dst_ref=bins.at[pl.ds(pl.multiple_of(tm * 32, 32), 32)],
            send_sem=bin_send,
            recv_sem=bin_recv,
            device_id=((tm + i) % 8, ch),
            device_id_type=MESH,
        ).start()

    for r in range(RADIX):
        tables[r].wait()

    for k in range(RADIX):
        r = (y + k) % 4
        re = lax.dot_general(tab[r], ya[r], NT, preferred_element_type=F32)
        spec[r, :, 0:CH, :] = re.astype(BF16).reshape(GROUP, CH, FR)
        im = lax.dot_general(tab[r], yb[r], NT, preferred_element_type=F32)
        spec[r, :, CH : 2 * CH, :] = im.astype(BF16).reshape(GROUP, CH, FR)

        @pl.loop(1 if k == 0 else 0, GROUP)
        def _(i):
            n = (i * 13) % GROUP
            to_tm, to_ch = partner(n % 4, n // 16, (n // 4) % 4, k)
            pltpu.make_async_remote_copy(
                src_ref=spec.at[r, to_tm * 4 + to_ch // 4],
                dst_ref=got.at[me],
                send_sem=spec_send,
                recv_sem=spec_recv,
                device_id=(to_tm, to_ch),
                device_id_type=MESH,
            ).start()

        if k == 0:
            got[me] = spec[r, tm * 4 + z]

    fill_mix(lags, mix)

    seven = pltpu.make_async_copy(bins.at[pl.ds(0, 224)], bins.at[pl.ds(0, 224)], bin_recv)
    seven.wait()
    high, low = table.at[pl.ds(0, 32)], table.at[pl.ds(32, 32)]
    frame_weights(bins, high, low, weight)
    fill_table(bins, weight, table)

    blocks = got.at[pl.ds(0, NDEV - 1)]
    pltpu.make_async_copy(blocks, blocks, spec_recv).wait()
    spread_spectra(got, xs)
    fold(lags, xs, table, prod_a, prod_b, acc)

    sums = acc[...].T
    exact = dict(preferred_element_type=F32, precision=lax.Precision.HIGHEST)
    res = jnp.dot(sums[0:NH], mix[0], **exact) + jnp.dot(sums[NH:], mix[1], **exact)
    for p in range(2):
        for half in range(2):
            mine[:, 2 * p + half, :] = res[p * 128 : (p + 1) * 128, half * 128 : (half + 1) * 128]

    @pl.loop(1, NDEV)
    def _(i):
        n = (i * 37) % NDEV
        to_tm, to_ch = partner(n % 4, n // 64, (n // 4) % 4, (n // 16) % 4)
        pltpu.make_async_remote_copy(
            src_ref=mine.at[to_tm * 16 + to_ch],
            dst_ref=theirs.at[me],
            send_sem=last_send,
            recv_sem=last_recv,
            device_id=(to_tm, to_ch),
            device_id_type=MESH,
        ).start()

    theirs[me] = mine[me]
    rest = theirs.at[pl.ds(0, NDEV - 1)]
    pltpu.make_async_copy(rest, rest, last_recv).wait()

    for p in range(2):
        for half in range(2):
            turned = theirs[:, 2 * p + half, :].T
            for j in range(CH // 2):
                for ro in range(2):
                    row = j * 16 + ro * 8
                    lanes = pl.ds((half * (CH // 2) + j) * 128, 128)
                    out[ro, p, :, lanes] = turned[row : row + 8]

    sent = bins.at[pl.ds(0, 224)]
    pltpu.make_async_copy(sent, sent, bin_send).wait()
    pltpu.make_async_copy(blocks, blocks, spec_send).wait()
    pltpu.make_async_copy(rest, rest, last_send).wait()


def on_device(samples, window_taper, phase_bins, lag_set):
    return pl.pallas_call(
        kernel,
        out_shape=jax.ShapeDtypeStruct((2, 2, L, K), F32),
        in_specs=[SMEM, ANY, VMEM, ANY, VMEM],
        out_specs=VMEM,
        scratch_shapes=[
            pltpu.VMEM((2, FR, K), F32),
            pltpu.VMEM((RADIX, K // RADIX, 2 * KR), BF16),
            pltpu.VMEM((RADIX, FR, 2 * KR), BF16),
            pltpu.VMEM((RADIX, FR, 2 * KR), BF16),
            pltpu.VMEM((RADIX, GROUP, 2 * CH, FR), BF16),
            pltpu.VMEM((NDEV, 2 * CH, FR), BF16),
            pltpu.VMEM((BLK, 128), jnp.int32),
            pltpu.VMEM((1, T), F32),
            pltpu.VMEM((BLK + PADBLK, 2 * CH, 128), BF16),
            pltpu.VMEM((2 * NH, T), BF16),
            pltpu.VMEM((L * 2 * CH, CHUNK * 128), BF16),
            pltpu.VMEM((L * 2 * CH, CHUNK * 128), BF16),
            pltpu.VMEM((L * 2 * CH, 2 * NH), F32),
            pltpu.VMEM((2, L * 2 * CH, CH * 2 * L), F32),
            pltpu.VMEM((NDEV, 4, 128), F32),
            pltpu.VMEM((NDEV, 4, 128), F32),
            pltpu.SemaphoreType.DMA((PARTS,)),
            pltpu.SemaphoreType.DMA((RADIX,)),
            pltpu.SemaphoreType.DMA,
            pltpu.SemaphoreType.DMA,
            pltpu.SemaphoreType.DMA,
            pltpu.SemaphoreType.DMA,
            pltpu.SemaphoreType.DMA,
            pltpu.SemaphoreType.DMA,
        ],
        compiler_params=pltpu.CompilerParams(
            vmem_limit_bytes=62 * 2**20, collective_id=0, has_side_effects=True
        ),
        name="cyclic",
    )(lag_set, samples, window_taper.reshape(1, K), jnp.asarray(chan_tables()), phase_bins.reshape(-1, 128))


def solution(mesh):
    placed = (P(None, ("tm", "chan"), None), P(), P("tm"), P())
    return jax.shard_map(
        on_device,
        mesh=mesh,
        in_specs=placed,
        out_specs=P(None, ("tm", "chan"), None, None),
        check_vma=False,
    )
```

```python
import math

import jax
import jax.numpy as jnp
import ml_dtypes
import numpy as np
from jax import lax
from jax.experimental import pallas as pl
from jax.experimental.pallas import tpu as pltpu
from jax.sharding import PartitionSpec as P

K = 2048
NB = 1024
NH = 256
L = 8
MAXLAG = 1024
T = 32768
NDEV = 128
FR = T // NDEV
CH = K // NDEV
RADIX = 4
KR = K // RADIX
GROUP = NDEV // RADIX
BLK = T // 128
PADBLK = 32
CHUNK = 8
STEPS = BLK // CHUNK
PARTS = 4
WIDE = 4
F32 = jnp.float32
BF16 = jnp.bfloat16
NT = (((1,), (1,)), ((), ()))
VMEM = pl.BlockSpec(memory_space=pltpu.VMEM)
SMEM = pl.BlockSpec(memory_space=pltpu.SMEM)
ANY = pl.BlockSpec(memory_space=pl.ANY)
MESH = pl.DeviceIdType.MESH


def exchange_order():
    hops = (0, 1, 2, 1)
    offsets = [(n % 4, n // 64, (n // 4) % 4, (n // 16) % 4) for n in (i * 37 % NDEV for i in range(1, NDEV))]
    return sorted(offsets, key=lambda o: (phase_of(o), -hops[o[0]] - hops[o[2]] - hops[o[3]]))


def phase_of(offset):
    return 2 * (offset[0] % 2) + offset[1]


ORDER = exchange_order()


def chan_tables():
    r = np.arange(RADIX)[:, None, None]
    i = np.arange(GROUP)[None, :, None]
    j = np.arange(CH)[None, None, :]
    chan = (NDEV * j + RADIX * i + r).reshape(-1)
    angle = (chan[:, None] * np.arange(KR)[None, :] % K) * (2.0 * math.pi / K)
    both = np.concatenate([np.cos(angle), np.sin(angle)], 1).astype(np.float32) * np.float32(1.0 / math.sqrt(K))
    return both.astype(ml_dtypes.bfloat16).reshape(RADIX, K // RADIX, 2 * KR)


def butterflies(held, taper, ya, yb, part):
    rows = FR // PARTS

    @pl.loop(0, rows // 16)
    def _(g):
        at = pl.ds(pl.multiple_of(part * rows + g * 16, 16), 16)
        for b in range(KR // 128):
            x = []
            for m in range(RADIX):
                lanes = pl.ds(m * KR + b * 128, 128)
                w = taper[:, lanes]
                x.append([(held[c, at, lanes] * w).astype(BF16).astype(F32) for c in range(2)])
            er, ei = x[0][0] + x[2][0], x[0][1] + x[2][1]
            fr, fi = x[1][0] + x[3][0], x[1][1] + x[3][1]
            gr, gi = x[0][0] - x[2][0], x[0][1] - x[2][1]
            hr, hi = x[1][0] - x[3][0], x[1][1] - x[3][1]
            y = [(er + fr, ei + fi), (gr + hi, gi - hr), (er - fr, ei - fi), (gr - hi, gi + hr)]
            for r in range(RADIX):
                re, im = y[r][0].astype(BF16), y[r][1].astype(BF16)
                ya[r, at, pl.ds(b * 128, 128)] = re
                ya[r, at, pl.ds(KR + b * 128, 128)] = im
                yb[r, at, pl.ds(b * 128, 128)] = im
                yb[r, at, pl.ds(KR + b * 128, 128)] = -re


def sincos(m, period):
    x = (m - period // 2).astype(F32) * (math.pi / period)
    z = x * x
    s = x * (1.0 + z * (-1.0 / 6 + z * (1.0 / 120 + z * (-1.0 / 5040 + z * (1.0 / 362880 - z / 39916800)))))
    c = 1.0 + z * (-0.5 + z * (1.0 / 24 + z * (-1.0 / 720 + z * (1.0 / 40320 + z * (-1.0 / 3628800 + z / 479001600)))))
    return 2.0 * s * s - 1.0, -2.0 * s * c


def rotated(e, f):
    return e[0] * f[0] - e[1] * f[1], e[0] * f[1] + e[1] * f[0]


def bins_of(bins, first):
    return jnp.concatenate([bins[pl.ds(first + i, 1), :] for i in range(WIDE)], 1)


def frame_weights(bins, high, low, weight):
    span = WIDE * 128
    row32 = lax.broadcasted_iota(jnp.int32, (32, span), 0)

    @pl.loop(0, BLK // WIDE)
    def _(m):
        b = bins_of(bins, m * WIDE)
        lanes = pl.ds(pl.multiple_of(m * span, span), span)
        high[:, lanes] = ((b >> 5) == row32).astype(F32).astype(BF16)
        low[:, lanes] = ((b & 31) == row32).astype(F32).astype(BF16)

    part = 4096
    hist = jnp.zeros((32, 32), F32)
    for p in range(T // part):
        lanes = pl.ds(p * part, part)
        hist = hist + lax.dot_general(high[:, lanes], low[:, lanes], NT, preferred_element_type=F32)
    inverse = (1.0 / math.sqrt(NB)) / jnp.maximum(hist, 1.0)
    first = inverse.astype(BF16)
    second = (inverse - first.astype(F32)).astype(BF16)

    @pl.loop(0, T // 1024)
    def _(p):
        lanes = pl.ds(pl.multiple_of(p * 1024, 1024), 1024)
        rows = jnp.dot(first, low[:, lanes], preferred_element_type=F32) + jnp.dot(
            second, low[:, lanes], preferred_element_type=F32
        )
        weight[:, lanes] = jnp.sum(rows * high[:, lanes].astype(F32), axis=0, keepdims=True)


def fill_table(bins, weight, table):
    span = WIDE * 128
    odd = 2 * lax.broadcasted_iota(jnp.int32, (8, span), 0) + 1

    @pl.loop(0, BLK // WIDE)
    def _(m):
        b = bins_of(bins, m * WIDE)
        lanes = pl.ds(pl.multiple_of(m * span, span), span)
        w = weight[:, lanes]
        c, s = sincos((odd * b) & (NB - 1), NB)
        one = (c[0:1], s[0:1])
        even = rotated((c, s), one)
        turn = (even[0][7:8], even[1][7:8])
        twice = 2.0 * turn[0]
        for parity, start in ((0, (c, s)), (1, even)):
            before = (start[0] * w, start[1] * w)
            now = rotated(before, turn)
            for g in range(8):
                for k in range(2):
                    rows = pl.ds(k * NH + parity * 128 + g * 16, 16)
                    table[rows, lanes] = jnp.concatenate([before[k], now[k]], 0).astype(BF16)
                if g < 7:
                    after = (twice * now[0] - before[0], twice * now[1] - before[1])
                    later = (twice * after[0] - now[0], twice * after[1] - now[1])
                    before, now = after, later


def fill_mix(lags, mix):
    shape = (2 * CH, CH * 2 * L)
    row = lax.broadcasted_iota(jnp.int32, shape, 0)
    col = lax.broadcasted_iota(jnp.int32, shape, 1)
    part_in, chan_in = row >> 4, row & 15
    chan_out, part_out, q = col >> 4, (col >> 3) & 1, col & 7
    here = jnp.where(chan_in == chan_out, 1.0 / math.sqrt(L), 0.0)
    same = part_in == part_out
    sign = jnp.where(part_in == 0, -1.0, 1.0)
    for l in range(L):
        c, s = sincos((lags[l] * q) & (2 * MAXLAG - 1), 2 * MAXLAG)
        rows = pl.ds(l * 2 * CH, 2 * CH)
        mix[0, rows, :] = here * jnp.where(same, c, sign * s)
        mix[1, rows, :] = here * jnp.where(same, -s, sign * c)


def spread_spectra(got, xs, first):
    @pl.loop(0, 4)
    def _(g):
        for e in range(4):
            s = first + g * 4 + e
            xs[2 * s] = got[s, :, 0:128]
            xs[2 * s + 1] = got[s, :, 128:256]


def fold(lags, xs, table, prod_a, prod_b, acc, step_at, count):
    lane = lax.broadcasted_iota(jnp.int32, (CH, 128), 1)

    def products(step, prod):
        first = step * CHUNK
        for l in range(L):
            lag = lags[l]
            whole, rest = lag >> 7, lag & 127
            back = (128 - rest) & 127
            inside = lane < 128 - rest
            moved = None
            for b in range(CHUNK + 1):
                there = xs[first + b + whole]
                ahead = [pltpu.roll(there[k * CH : (k + 1) * CH], back, 1).astype(F32) for k in range(2)]
                if b > 0:
                    here = xs[first + b - 1].astype(F32)
                    re, im = here[0:CH], here[CH : 2 * CH]
                    lre = jnp.where(inside, moved[0], ahead[0])
                    lim = jnp.where(inside, moved[1], ahead[1])
                    lanes = pl.ds((b - 1) * 128, 128)
                    prod[pl.ds(l * 2 * CH, CH), lanes] = (re * lre + im * lim).astype(BF16)
                    prod[pl.ds(l * 2 * CH + CH, CH), lanes] = (im * lre - re * lim).astype(BF16)
                moved = ahead

    def add(step, prod):
        lanes = pl.ds(pl.multiple_of(step * CHUNK * 128, CHUNK * 128), CHUNK * 128)
        acc[...] += lax.dot_general(prod[...], table[:, lanes], NT, preferred_element_type=F32)

    products(step_at(0), prod_a)

    @pl.loop(0, count // 2 - 1)
    def _(i):
        add(step_at(2 * i), prod_a)
        products(step_at(2 * i + 1), prod_b)
        add(step_at(2 * i + 1), prod_b)
        products(step_at(2 * i + 2), prod_a)

    add(step_at(count - 2), prod_a)
    products(step_at(count - 1), prod_b)
    add(step_at(count - 1), prod_b)


def kernel(
    lags, samples, taper, chans, own_bins, out,
    held, tab, ya, yb, spec, got, bins, weight, xs, table, prod_a, prod_b, acc, mix, mine, theirs,
    sem_s, sem_t, bin_send, bin_recv, spec_send, spec_recv, last_send, last_recv,
):
    tm, ch = lax.axis_index("tm"), lax.axis_index("chan")
    me = tm * 16 + ch
    x, core, z, y = tm // 2, tm % 2, ch // 4, ch % 4

    def partner(dx, dc, dz, dy):
        return ((x + dx) % 4) * 2 + (core + dc) % 2, ((z + dz) % 4) * 4 + (y + dy) % 4

    barrier = pltpu.get_barrier_semaphore()

    rows = FR // PARTS
    loads = []
    for p in range(PARTS):
        part = pl.ds(p * rows, rows)
        loads.append(pltpu.make_async_copy(samples.at[:, part], held.at[:, part], sem_s.at[p]))
        loads[-1].start()
    tables = []
    for r in range(RADIX):
        tables.append(pltpu.make_async_copy(chans.at[r], tab.at[r], sem_t.at[r]))
        tables[-1].start()

    @pl.loop(1, NDEV)
    def _(i):
        to = (me + i) % NDEV
        pl.semaphore_signal(barrier, inc=1, device_id=(to // 16, to % 16), device_id_type=MESH)

    for p in range(PARTS):
        loads[p].wait()
        butterflies(held, taper, ya, yb, p)

    for r in range(RADIX):
        tables[r].wait()
        re = lax.dot_general(tab[r], ya[r], NT, preferred_element_type=F32)
        spec[r, :, 0:CH, :] = re.astype(BF16).reshape(GROUP, CH, FR)
        im = lax.dot_general(tab[r], yb[r], NT, preferred_element_type=F32)
        spec[r, :, CH : 2 * CH, :] = im.astype(BF16).reshape(GROUP, CH, FR)

    pl.semaphore_wait(barrier, NDEV - 1)

    bins[pl.ds(pl.multiple_of(tm * 32, 32), 32), :] = own_bins[...]

    @pl.loop(1, 8)
    def _(i):
        pltpu.make_async_remote_copy(
            src_ref=own_bins,
            dst_ref=bins.at[pl.ds(pl.multiple_of(tm * 32, 32), 32)],
            send_sem=bin_send,
            recv_sem=bin_recv,
            device_id=((tm + i) % 8, ch),
            device_id_type=MESH,
        ).start()

    for dx, dc, dz, dy in ORDER:
        to_tm, to_ch = partner(dx, dc, dz, dy)
        pltpu.make_async_remote_copy(
            src_ref=spec.at[(y + dy) % 4, to_tm * 4 + to_ch // 4],
            dst_ref=got.at[me],
            send_sem=spec_send,
            recv_sem=spec_recv.at[phase_of((dx, dc, dz, dy))],
            device_id=(to_tm, to_ch),
            device_id_type=MESH,
        ).start()

    got[me] = spec[y, tm * 4 + z]

    fill_mix(lags, mix)

    seven = pltpu.make_async_copy(bins.at[pl.ds(0, 224)], bins.at[pl.ds(0, 224)], bin_recv)
    seven.wait()
    high, low = table.at[pl.ds(0, 32)], table.at[pl.ds(32, 32)]
    frame_weights(bins, high, low, weight)
    fill_table(bins, weight, table)

    acc[...] = jnp.zeros_like(acc)
    xs[pl.ds(BLK, PADBLK)] = jnp.zeros((PADBLK, 2 * CH, 128), BF16)

    def step_of(at_x, at_core, at_z):
        return (at_x % 4) * 8 + at_core * 4 + at_z

    def inner(shift, at_core):
        return lambda i: step_of(x + shift + 2 * (i // 3), at_core, i % 3)

    def with_last(start, shift, last_core):
        def step_at(i):
            late = i // 6
            k = i - 6
            return (1 - late) * start(i) + late * step_of(x + shift + 2 * (k % 2), last_core, 3)

        return step_at

    def with_all(start):
        def step_at(i):
            late = i // 6
            k = i - 6
            odd = k // 2
            end = (1 - odd) * step_of(x + 1 + 2 * (k % 2), 0, 3) + odd * step_of(x + 1 - core + 2 * (k % 2), 1, 3)
            return (1 - late) * start(i) + late * end

        return step_at

    phases = (
        (0, core, inner(0, core), 6),
        (0, 1 - core, with_last(inner(0, 1 - core), 0, 0), 8),
        (1, core, with_last(inner(1, core), core, 1), 8),
        (1, 1 - core, with_all(inner(1, 1 - core)), 10),
    )
    for phase, (shift, at_core, step_at, count) in enumerate(phases):
        came = got.at[pl.ds(0, 31 if phase == 0 else 32)]
        pltpu.make_async_copy(came, came, spec_recv.at[phase]).wait()
        for k in range(2):
            spread_spectra(got, xs, ((x + shift + 2 * k) % 4) * 32 + at_core * 16)
        fold(lags, xs, table, prod_a, prod_b, acc, step_at, count)

    sums = acc[...].T
    exact = dict(preferred_element_type=F32, precision=lax.Precision.HIGHEST)
    res = jnp.dot(sums[0:NH], mix[0], **exact) + jnp.dot(sums[NH:], mix[1], **exact)
    for p in range(2):
        for half in range(2):
            mine[:, 2 * p + half, :] = res[p * 128 : (p + 1) * 128, half * 128 : (half + 1) * 128]

    @pl.loop(1, NDEV)
    def _(i):
        n = (i * 37) % NDEV
        to_tm, to_ch = partner(n % 4, n // 64, (n // 4) % 4, (n // 16) % 4)
        pltpu.make_async_remote_copy(
            src_ref=mine.at[to_tm * 16 + to_ch],
            dst_ref=theirs.at[me],
            send_sem=last_send,
            recv_sem=last_recv,
            device_id=(to_tm, to_ch),
            device_id_type=MESH,
        ).start()

    theirs[me] = mine[me]
    rest = theirs.at[pl.ds(0, NDEV - 1)]
    pltpu.make_async_copy(rest, rest, last_recv).wait()

    for p in range(2):
        for half in range(2):
            turned = theirs[:, 2 * p + half, :].T
            for j in range(CH // 2):
                for ro in range(2):
                    row = j * 16 + ro * 8
                    lanes = pl.ds((half * (CH // 2) + j) * 128, 128)
                    out[ro, p, :, lanes] = turned[row : row + 8]

    sent = bins.at[pl.ds(0, 224)]
    pltpu.make_async_copy(sent, sent, bin_send).wait()
    blocks = got.at[pl.ds(0, NDEV - 1)]
    pltpu.make_async_copy(blocks, blocks, spec_send).wait()
    pltpu.make_async_copy(rest, rest, last_send).wait()


def on_device(samples, window_taper, phase_bins, lag_set):
    return pl.pallas_call(
        kernel,
        out_shape=jax.ShapeDtypeStruct((2, 2, L, K), F32),
        in_specs=[SMEM, ANY, VMEM, ANY, VMEM],
        out_specs=VMEM,
        scratch_shapes=[
            pltpu.VMEM((2, FR, K), F32),
            pltpu.VMEM((RADIX, K // RADIX, 2 * KR), BF16),
            pltpu.VMEM((RADIX, FR, 2 * KR), BF16),
            pltpu.VMEM((RADIX, FR, 2 * KR), BF16),
            pltpu.VMEM((RADIX, GROUP, 2 * CH, FR), BF16),
            pltpu.VMEM((NDEV, 2 * CH, FR), BF16),
            pltpu.VMEM((BLK, 128), jnp.int32),
            pltpu.VMEM((1, T), F32),
            pltpu.VMEM((BLK + PADBLK, 2 * CH, 128), BF16),
            pltpu.VMEM((2 * NH, T), BF16),
            pltpu.VMEM((L * 2 * CH, CHUNK * 128), BF16),
            pltpu.VMEM((L * 2 * CH, CHUNK * 128), BF16),
            pltpu.VMEM((L * 2 * CH, 2 * NH), F32),
            pltpu.VMEM((2, L * 2 * CH, CH * 2 * L), F32),
            pltpu.VMEM((NDEV, 4, 128), F32),
            pltpu.VMEM((NDEV, 4, 128), F32),
            pltpu.SemaphoreType.DMA((PARTS,)),
            pltpu.SemaphoreType.DMA((RADIX,)),
            pltpu.SemaphoreType.DMA,
            pltpu.SemaphoreType.DMA,
            pltpu.SemaphoreType.DMA,
            pltpu.SemaphoreType.DMA((4,)),
            pltpu.SemaphoreType.DMA,
            pltpu.SemaphoreType.DMA,
        ],
        compiler_params=pltpu.CompilerParams(
            vmem_limit_bytes=62 * 2**20, collective_id=0, has_side_effects=True
        ),
        name="cyclic",
    )(lag_set, samples, window_taper.reshape(1, K), jnp.asarray(chan_tables()), phase_bins.reshape(-1, 128))


def solution(mesh):
    placed = (P(None, ("tm", "chan"), None), P(), P("tm"), P())
    return jax.shard_map(
        on_device,
        mesh=mesh,
        in_specs=placed,
        out_specs=P(None, ("tm", "chan"), None, None),
        check_vma=False,
    )
```

```python
import math

import jax
import jax.numpy as jnp
import ml_dtypes
import numpy as np
from jax import lax
from jax.experimental import pallas as pl
from jax.experimental.pallas import tpu as pltpu
from jax.sharding import PartitionSpec as P

K = 2048
NB = 1024
NH = 256
L = 8
MAXLAG = 1024
T = 32768
NDEV = 128
FR = T // NDEV
CH = K // NDEV
RADIX = 4
KR = K // RADIX
GROUP = NDEV // RADIX
BLK = T // 128
PADBLK = 32
CHUNK = 8
STEPS = BLK // CHUNK
PARTS = 4
WIDE = 4
F32 = jnp.float32
BF16 = jnp.bfloat16
NT = (((1,), (1,)), ((), ()))
VMEM = pl.BlockSpec(memory_space=pltpu.VMEM)
SMEM = pl.BlockSpec(memory_space=pltpu.SMEM)
ANY = pl.BlockSpec(memory_space=pl.ANY)
MESH = pl.DeviceIdType.MESH


def exchange_order():
    hops = (0, 1, 2, 1)
    offsets = [(n % 4, n // 64, (n // 4) % 4, (n // 16) % 4) for n in (i * 37 % NDEV for i in range(1, NDEV))]
    return sorted(offsets, key=lambda o: (phase_of(o), -hops[o[0]] - hops[o[2]] - hops[o[3]]))


def phase_of(offset):
    return 2 * (offset[0] % 2) + offset[1]


ORDER = exchange_order()


def chan_tables():
    r = np.arange(RADIX)[:, None, None]
    i = np.arange(GROUP)[None, :, None]
    j = np.arange(CH)[None, None, :]
    chan = (NDEV * j + RADIX * i + r).reshape(-1)
    angle = (chan[:, None] * np.arange(KR)[None, :] % K) * (2.0 * math.pi / K)
    both = np.concatenate([np.cos(angle), np.sin(angle)], 1).astype(np.float32) * np.float32(1.0 / math.sqrt(K))
    return both.astype(ml_dtypes.bfloat16).reshape(RADIX, K // RADIX, 2 * KR)


def butterflies(held, taper, ya, yb, part):
    rows = FR // PARTS

    @pl.loop(0, rows // 16)
    def _(g):
        at = pl.ds(pl.multiple_of(part * rows + g * 16, 16), 16)
        for b in range(KR // 128):
            x = []
            for m in range(RADIX):
                lanes = pl.ds(m * KR + b * 128, 128)
                w = taper[:, lanes]
                x.append([(held[c, at, lanes] * w).astype(BF16).astype(F32) for c in range(2)])
            er, ei = x[0][0] + x[2][0], x[0][1] + x[2][1]
            fr, fi = x[1][0] + x[3][0], x[1][1] + x[3][1]
            gr, gi = x[0][0] - x[2][0], x[0][1] - x[2][1]
            hr, hi = x[1][0] - x[3][0], x[1][1] - x[3][1]
            y = [(er + fr, ei + fi), (gr + hi, gi - hr), (er - fr, ei - fi), (gr - hi, gi + hr)]
            for r in range(RADIX):
                re, im = y[r][0].astype(BF16), y[r][1].astype(BF16)
                ya[r, at, pl.ds(b * 128, 128)] = re
                ya[r, at, pl.ds(KR + b * 128, 128)] = im
                yb[r, at, pl.ds(b * 128, 128)] = im
                yb[r, at, pl.ds(KR + b * 128, 128)] = -re


def sincos(m, period):
    x = (m - period // 2).astype(F32) * (math.pi / period)
    z = x * x
    s = x * (1.0 + z * (-1.0 / 6 + z * (1.0 / 120 + z * (-1.0 / 5040 + z * (1.0 / 362880 - z / 39916800)))))
    c = 1.0 + z * (-0.5 + z * (1.0 / 24 + z * (-1.0 / 720 + z * (1.0 / 40320 + z * (-1.0 / 3628800 + z / 479001600)))))
    return 2.0 * s * s - 1.0, -2.0 * s * c


def rotated(e, f):
    return e[0] * f[0] - e[1] * f[1], e[0] * f[1] + e[1] * f[0]


def bins_of(bins, first, count):
    return jnp.concatenate([bins[pl.ds(first + i, 1), :] for i in range(count)], 1)


def frame_weights(bins, high, low, weight):
    span = 8 * 128
    row32 = lax.broadcasted_iota(jnp.int32, (32, span), 0)

    @pl.loop(0, BLK // 8)
    def _(m):
        b = bins_of(bins, m * 8, 8)
        lanes = pl.ds(pl.multiple_of(m * span, span), span)
        high[:, lanes] = ((b >> 5) == row32).astype(F32).astype(BF16)
        ones = ((b & 31) == row32).astype(F32).astype(BF16)
        low[0:32, lanes] = ones
        low[32:64, lanes] = ones

    part = 4096
    hist = jnp.zeros((32, 32), F32)
    for p in range(T // part):
        lanes = pl.ds(p * part, part)
        hist = hist + lax.dot_general(high[:, lanes], low[0:32, lanes], NT, preferred_element_type=F32)
    inverse = (1.0 / math.sqrt(NB)) / jnp.maximum(hist, 1.0)
    first = inverse.astype(BF16)
    second = (inverse - first.astype(F32)).astype(BF16)
    both = jnp.concatenate([first, second], 1)

    for p in range(T // part):
        lanes = pl.ds(p * part, part)
        rows = jnp.dot(both, low[:, lanes], preferred_element_type=F32)
        weight[:, lanes] = jnp.sum(rows * high[:, lanes].astype(F32), axis=0, keepdims=True)


def fill_table(bins, weight, table, beside):
    span = WIDE * 128
    odd = 2 * lax.broadcasted_iota(jnp.int32, (8, span), 0) + 1

    @pl.loop(0, BLK // WIDE)
    def _(m):
        beside(m)
        b = bins_of(bins, m * WIDE, WIDE)
        lanes = pl.ds(pl.multiple_of(m * span, span), span)
        w = weight[:, lanes]
        c, s = sincos((odd * b) & (NB - 1), NB)
        one = (c[0:1], s[0:1])
        even = rotated((c, s), one)
        turn = (even[0][7:8], even[1][7:8])
        twice = 2.0 * turn[0]
        for parity, start in ((0, (c, s)), (1, even)):
            before = (start[0] * w, start[1] * w)
            now = rotated(before, turn)
            for g in range(8):
                for k in range(2):
                    rows = pl.ds(k * NH + parity * 128 + g * 16, 16)
                    table[rows, lanes] = jnp.concatenate([before[k], now[k]], 0).astype(BF16)
                if g < 7:
                    after = (twice * now[0] - before[0], twice * now[1] - before[1])
                    later = (twice * after[0] - now[0], twice * after[1] - now[1])
                    before, now = after, later


def fill_mix(lags, mix):
    shape = (2 * CH, CH * 2 * L)
    row = lax.broadcasted_iota(jnp.int32, shape, 0)
    col = lax.broadcasted_iota(jnp.int32, shape, 1)
    part_in, chan_in = row >> 4, row & 15
    chan_out, part_out, q = col >> 4, (col >> 3) & 1, col & 7
    here = jnp.where(chan_in == chan_out, 1.0 / math.sqrt(L), 0.0)
    same = part_in == part_out
    sign = jnp.where(part_in == 0, -1.0, 1.0)
    for l in range(L):
        c, s = sincos((lags[l] * q) & (2 * MAXLAG - 1), 2 * MAXLAG)
        rows = pl.ds(l * 2 * CH, 2 * CH)
        mix[0, rows, :] = here * jnp.where(same, c, sign * s)
        mix[1, rows, :] = here * jnp.where(same, -s, sign * c)


def spread_spectra(got, xs, first):
    @pl.loop(0, 4)
    def _(g):
        for e in range(4):
            s = first + g * 4 + e
            xs[2 * s] = got[s, :, 0:128]
            xs[2 * s + 1] = got[s, :, 128:256]


def fold(lags, xs, table, prod_a, prod_b, acc, step_at, count):
    lane = lax.broadcasted_iota(jnp.int32, (CH, 128), 1)

    def products(step, prod):
        first = step * CHUNK
        for l in range(L):
            lag = lags[l]
            whole, rest = lag >> 7, lag & 127
            back = (128 - rest) & 127
            inside = lane < 128 - rest
            moved = None
            for b in range(CHUNK + 1):
                there = xs[first + b + whole]
                ahead = [pltpu.roll(there[k * CH : (k + 1) * CH], back, 1).astype(F32) for k in range(2)]
                if b > 0:
                    here = xs[first + b - 1].astype(F32)
                    re, im = here[0:CH], here[CH : 2 * CH]
                    lre = jnp.where(inside, moved[0], ahead[0])
                    lim = jnp.where(inside, moved[1], ahead[1])
                    lanes = pl.ds((b - 1) * 128, 128)
                    prod[pl.ds(l * 2 * CH, CH), lanes] = (re * lre + im * lim).astype(BF16)
                    prod[pl.ds(l * 2 * CH + CH, CH), lanes] = (im * lre - re * lim).astype(BF16)
                moved = ahead

    def add(step, prod):
        lanes = pl.ds(pl.multiple_of(step * CHUNK * 128, CHUNK * 128), CHUNK * 128)
        acc[...] += lax.dot_general(prod[...], table[:, lanes], NT, preferred_element_type=F32)

    products(step_at(0), prod_a)

    @pl.loop(0, count // 2 - 1)
    def _(i):
        add(step_at(2 * i), prod_a)
        products(step_at(2 * i + 1), prod_b)
        add(step_at(2 * i + 1), prod_b)
        products(step_at(2 * i + 2), prod_a)

    add(step_at(count - 2), prod_a)
    products(step_at(count - 1), prod_b)
    add(step_at(count - 1), prod_b)


def kernel(
    lags, samples, taper, chans, own_bins, out,
    held, tab, ya, yb, spec, got, bins, weight, xs, table, prod_a, prod_b, acc, mix, mine, mid, theirs,
    sem_s, sem_t, bin_send, bin_recv, spec_send, spec_recv, mid_send, mid_recv, last_send, last_recv,
):
    tm, ch = lax.axis_index("tm"), lax.axis_index("chan")
    me = tm * 16 + ch
    x, core, z, y = tm // 2, tm % 2, ch // 4, ch % 4

    def partner(dx, dc, dz, dy):
        return ((x + dx) % 4) * 2 + (core + dc) % 2, ((z + dz) % 4) * 4 + (y + dy) % 4

    barrier = pltpu.get_barrier_semaphore()

    rows = FR // PARTS
    loads = []
    for p in range(PARTS):
        part = pl.ds(p * rows, rows)
        loads.append(pltpu.make_async_copy(samples.at[:, part], held.at[:, part], sem_s.at[p]))
        loads[-1].start()
    tables = []
    for r in range(RADIX):
        tables.append(pltpu.make_async_copy(chans.at[r], tab.at[r], sem_t.at[r]))
        tables[-1].start()

    @pl.loop(1, NDEV)
    def _(i):
        to = (me + i) % NDEV
        pl.semaphore_signal(barrier, inc=1, device_id=(to // 16, to % 16), device_id_type=MESH)

    for p in range(PARTS):
        loads[p].wait()
        butterflies(held, taper, ya, yb, p)

    for r in range(RADIX):
        tables[r].wait()
        re = lax.dot_general(tab[r], ya[r], NT, preferred_element_type=F32)
        spec[r, :, 0:CH, :] = re.astype(BF16).reshape(GROUP, CH, FR)
        im = lax.dot_general(tab[r], yb[r], NT, preferred_element_type=F32)
        spec[r, :, CH : 2 * CH, :] = im.astype(BF16).reshape(GROUP, CH, FR)

    pl.semaphore_wait(barrier, NDEV - 1)

    bins[pl.ds(pl.multiple_of(tm * 32, 32), 32), :] = own_bins[...]

    @pl.loop(1, 8)
    def _(i):
        pltpu.make_async_remote_copy(
            src_ref=own_bins,
            dst_ref=bins.at[pl.ds(pl.multiple_of(tm * 32, 32), 32)],
            send_sem=bin_send,
            recv_sem=bin_recv,
            device_id=((tm + i) % 8, ch),
            device_id_type=MESH,
        ).start()

    def send_spectra(offset, phase):
        to_tm, to_ch = partner(*offset)
        pltpu.make_async_remote_copy(
            src_ref=spec.at[(y + offset[3]) % 4, to_tm * 4 + to_ch // 4],
            dst_ref=got.at[me],
            send_sem=spec_send,
            recv_sem=spec_recv.at[phase],
            device_id=(to_tm, to_ch),
            device_id_type=MESH,
        ).start()

    for offset in ORDER:
        if phase_of(offset) < 2:
            send_spectra(offset, phase_of(offset))

    got[me] = spec[y, tm * 4 + z]

    fill_mix(lags, mix)

    seven = pltpu.make_async_copy(bins.at[pl.ds(0, 224)], bins.at[pl.ds(0, 224)], bin_recv)
    seven.wait()
    high, low = table.at[pl.ds(0, 32)], table.at[pl.ds(32, 64)]
    frame_weights(bins, high, low, weight)

    def send_beside(m):
        late = m // 32
        n = (m * 13) % 32
        send_spectra((1 + 2 * (n % 2), late, (n // 2) % 4, n // 8), 2 + late)

    fill_table(bins, weight, table, send_beside)

    acc[...] = jnp.zeros_like(acc)
    xs[pl.ds(BLK, PADBLK)] = jnp.zeros((PADBLK, 2 * CH, 128), BF16)

    def step_of(at_x, at_core, at_z):
        return (at_x % 4) * 8 + at_core * 4 + at_z

    def first_steps(i):
        return step_of(x + 2 * (i // 7), 0, i % 7)

    def inner(at_core):
        return lambda i: step_of(x + 1 + 2 * (i // 3), at_core, i % 3)

    def third_steps(i):
        late = i // 6
        return (1 - late) * inner(core)(i) + late * step_of(x + core + 2 * (i % 2), 1, 3)

    def fourth_steps(i):
        late, odd = i // 6, i // 8
        end = (1 - odd) * step_of(x + 1 + 2 * (i % 2), 0, 3) + odd * step_of(x + 1 - core + 2 * (i % 2), 1, 3)
        return (1 - late) * inner(1 - core)(i) + late * end

    for phase in range(4):
        shift, at_core = phase // 2, core if phase % 2 == 0 else 1 - core
        came = got.at[pl.ds(0, 31 if phase == 0 else 32)]
        pltpu.make_async_copy(came, came, spec_recv.at[phase]).wait()
        for k in range(2):
            spread_spectra(got, xs, ((x + shift + 2 * k) % 4) * 32 + at_core * 16)
        if phase > 0:
            step_at, count = ((first_steps, 14), (third_steps, 8), (fourth_steps, 10))[phase - 1]
            fold(lags, xs, table, prod_a, prod_b, acc, step_at, count)

    sums = acc[...].T
    exact = dict(preferred_element_type=F32, precision=lax.Precision.HIGHEST)
    res = jnp.dot(sums[0:NH], mix[0], **exact) + jnp.dot(sums[NH:], mix[1], **exact)
    for p in range(2):
        for half in range(2):
            rows = res[p * 128 : (p + 1) * 128, half * 128 : (half + 1) * 128]
            mine[:, :, 2 * p + half, :] = rows.reshape(8, 16, 128)

    for i in range(1, 8):
        to_tm = (tm + i) % 8
        pltpu.make_async_remote_copy(
            src_ref=mine.at[to_tm],
            dst_ref=mid.at[tm],
            send_sem=mid_send,
            recv_sem=mid_recv,
            device_id=(to_tm, ch),
            device_id_type=MESH,
        ).start()
    mid[tm] = mine[tm]
    some = mid.at[pl.ds(0, 7)]
    pltpu.make_async_copy(some, some, mid_recv).wait()
    for i in range(1, 16):
        to_ch = (ch + i) % 16
        pltpu.make_async_remote_copy(
            src_ref=mid.at[:, to_ch],
            dst_ref=theirs.at[:, ch],
            send_sem=last_send,
            recv_sem=last_recv,
            device_id=(tm, to_ch),
            device_id_type=MESH,
        ).start()
    theirs[:, ch] = mid[:, ch]
    rest = theirs.at[:, pl.ds(0, 15)]
    pltpu.make_async_copy(rest, rest, last_recv).wait()

    for p in range(2):
        for half in range(2):
            turned = theirs[:, :, 2 * p + half, :].reshape(NDEV, 128).T
            for j in range(CH // 2):
                for ro in range(2):
                    row = j * 16 + ro * 8
                    lanes = pl.ds((half * (CH // 2) + j) * 128, 128)
                    out[ro, p, :, lanes] = turned[row : row + 8]

    sent = bins.at[pl.ds(0, 224)]
    pltpu.make_async_copy(sent, sent, bin_send).wait()
    blocks = got.at[pl.ds(0, NDEV - 1)]
    pltpu.make_async_copy(blocks, blocks, spec_send).wait()
    pltpu.make_async_copy(some, some, mid_send).wait()
    pltpu.make_async_copy(rest, rest, last_send).wait()


def on_device(samples, window_taper, phase_bins, lag_set):
    return pl.pallas_call(
        kernel,
        out_shape=jax.ShapeDtypeStruct((2, 2, L, K), F32),
        in_specs=[SMEM, ANY, VMEM, ANY, VMEM],
        out_specs=VMEM,
        scratch_shapes=[
            pltpu.VMEM((2, FR, K), F32),
            pltpu.VMEM((RADIX, K // RADIX, 2 * KR), BF16),
            pltpu.VMEM((RADIX, FR, 2 * KR), BF16),
            pltpu.VMEM((RADIX, FR, 2 * KR), BF16),
            pltpu.VMEM((RADIX, GROUP, 2 * CH, FR), BF16),
            pltpu.VMEM((NDEV, 2 * CH, FR), BF16),
            pltpu.VMEM((BLK, 128), jnp.int32),
            pltpu.VMEM((1, T), F32),
            pltpu.VMEM((BLK + PADBLK, 2 * CH, 128), BF16),
            pltpu.VMEM((2 * NH, T), BF16),
            pltpu.VMEM((L * 2 * CH, CHUNK * 128), BF16),
            pltpu.VMEM((L * 2 * CH, CHUNK * 128), BF16),
            pltpu.VMEM((L * 2 * CH, 2 * NH), F32),
            pltpu.VMEM((2, L * 2 * CH, CH * 2 * L), F32),
            pltpu.VMEM((8, 16, 4, 128), F32),
            pltpu.VMEM((8, 16, 4, 128), F32),
            pltpu.VMEM((8, 16, 4, 128), F32),
            pltpu.SemaphoreType.DMA((PARTS,)),
            pltpu.SemaphoreType.DMA((RADIX,)),
            pltpu.SemaphoreType.DMA,
            pltpu.SemaphoreType.DMA,
            pltpu.SemaphoreType.DMA,
            pltpu.SemaphoreType.DMA((4,)),
            pltpu.SemaphoreType.DMA,
            pltpu.SemaphoreType.DMA,
            pltpu.SemaphoreType.DMA,
            pltpu.SemaphoreType.DMA,
        ],
        compiler_params=pltpu.CompilerParams(
            vmem_limit_bytes=62 * 2**20, collective_id=0, has_side_effects=True
        ),
        name="cyclic",
    )(lag_set, samples, window_taper.reshape(1, K), jnp.asarray(chan_tables()), phase_bins.reshape(-1, 128))


def solution(mesh):
    placed = (P(None, ("tm", "chan"), None), P(), P("tm"), P())
    return jax.shard_map(
        on_device,
        mesh=mesh,
        in_specs=placed,
        out_specs=P(None, ("tm", "chan"), None, None),
        check_vma=False,
    )
```

```python
import math

import jax
import jax.numpy as jnp
import ml_dtypes
import numpy as np
from jax import lax
from jax.experimental import pallas as pl
from jax.experimental.pallas import tpu as pltpu
from jax.sharding import PartitionSpec as P

K = 2048
NB = 1024
NH = 256
L = 8
MAXLAG = 1024
T = 32768
NDEV = 128
FR = T // NDEV
CH = K // NDEV
RADIX = 4
KR = K // RADIX
GROUP = NDEV // RADIX
BLK = T // 128
PADBLK = 32
CHUNK = 8
STEPS = BLK // CHUNK
PARTS = 4
WIDE = 4
F32 = jnp.float32
BF16 = jnp.bfloat16
NT = (((1,), (1,)), ((), ()))
VMEM = pl.BlockSpec(memory_space=pltpu.VMEM)
SMEM = pl.BlockSpec(memory_space=pltpu.SMEM)
ANY = pl.BlockSpec(memory_space=pl.ANY)
MESH = pl.DeviceIdType.MESH


def hops(offset):
    return sum((0, 1, 2, 1)[offset[axis]] for axis in (0, 2, 3))


def offsets():
    mixed = [(n % 4, n // 64, (n // 4) % 4, (n // 16) % 4) for n in (i * 37 % NDEV for i in range(1, NDEV))]
    return sorted(mixed, key=lambda offset: -hops(offset))


def phase_of(offset):
    return 2 * (offset[0] % 2) + offset[1]


LAST_ORDER = offsets()
FIRST_ORDER = [offset for offset in LAST_ORDER if phase_of(offset) == 0]


def chan_tables():
    r = np.arange(RADIX)[:, None, None]
    i = np.arange(GROUP)[None, :, None]
    j = np.arange(CH)[None, None, :]
    chan = (NDEV * j + RADIX * i + r).reshape(-1)
    angle = (chan[:, None] * np.arange(KR)[None, :] % K) * (2.0 * math.pi / K)
    both = np.concatenate([np.cos(angle), np.sin(angle)], 1).astype(np.float32) * np.float32(1.0 / math.sqrt(K))
    return both.astype(ml_dtypes.bfloat16).reshape(RADIX, K // RADIX, 2 * KR)


def butterflies(held, taper, ya, yb, part):
    rows = FR // PARTS

    @pl.loop(0, rows // 16)
    def _(g):
        at = pl.ds(pl.multiple_of(part * rows + g * 16, 16), 16)
        for b in range(KR // 128):
            x = []
            for m in range(RADIX):
                lanes = pl.ds(m * KR + b * 128, 128)
                w = taper[:, lanes]
                x.append([(held[c, at, lanes] * w).astype(BF16).astype(F32) for c in range(2)])
            er, ei = x[0][0] + x[2][0], x[0][1] + x[2][1]
            fr, fi = x[1][0] + x[3][0], x[1][1] + x[3][1]
            gr, gi = x[0][0] - x[2][0], x[0][1] - x[2][1]
            hr, hi = x[1][0] - x[3][0], x[1][1] - x[3][1]
            y = [(er + fr, ei + fi), (gr + hi, gi - hr), (er - fr, ei - fi), (gr - hi, gi + hr)]
            for r in range(RADIX):
                re, im = y[r][0].astype(BF16), y[r][1].astype(BF16)
                ya[r, at, pl.ds(b * 128, 128)] = re
                ya[r, at, pl.ds(KR + b * 128, 128)] = im
                yb[r, at, pl.ds(b * 128, 128)] = im
                yb[r, at, pl.ds(KR + b * 128, 128)] = -re


def sincos(m, period):
    x = (m - period // 2).astype(F32) * (math.pi / period)
    z = x * x
    s = x * (1.0 + z * (-1.0 / 6 + z * (1.0 / 120 + z * (-1.0 / 5040 + z * (1.0 / 362880 - z / 39916800)))))
    c = 1.0 + z * (-0.5 + z * (1.0 / 24 + z * (-1.0 / 720 + z * (1.0 / 40320 + z * (-1.0 / 3628800 + z / 479001600)))))
    return 2.0 * s * s - 1.0, -2.0 * s * c


def rotated(e, f):
    return e[0] * f[0] - e[1] * f[1], e[0] * f[1] + e[1] * f[0]


def bins_of(bins, first, count):
    return jnp.concatenate([bins[pl.ds(first + i, 1), :] for i in range(count)], 1)


def frame_weights(bins, high, low, weight, beside):
    span = 8 * 128
    row32 = lax.broadcasted_iota(jnp.int32, (32, span), 0)

    @pl.loop(0, BLK // 8)
    def _(m):
        beside(m)
        b = bins_of(bins, m * 8, 8)
        lanes = pl.ds(pl.multiple_of(m * span, span), span)
        high[:, lanes] = ((b >> 5) == row32).astype(F32).astype(BF16)
        ones = ((b & 31) == row32).astype(F32).astype(BF16)
        low[0:32, lanes] = ones
        low[32:64, lanes] = ones

    part = 4096
    hist = jnp.zeros((32, 32), F32)
    for p in range(T // part):
        lanes = pl.ds(p * part, part)
        hist = hist + lax.dot_general(high[:, lanes], low[0:32, lanes], NT, preferred_element_type=F32)
    inverse = (1.0 / math.sqrt(NB)) / jnp.maximum(hist, 1.0)
    first = inverse.astype(BF16)
    second = (inverse - first.astype(F32)).astype(BF16)
    both = jnp.concatenate([first, second], 1)

    for p in range(T // part):
        lanes = pl.ds(p * part, part)
        rows = jnp.dot(both, low[:, lanes], preferred_element_type=F32)
        weight[:, lanes] = jnp.sum(rows * high[:, lanes].astype(F32), axis=0, keepdims=True)


def fill_table(bins, weight, table, beside):
    span = WIDE * 128
    odd = 2 * lax.broadcasted_iota(jnp.int32, (8, span), 0) + 1

    @pl.loop(0, BLK // WIDE)
    def _(m):
        beside(m)
        b = bins_of(bins, m * WIDE, WIDE)
        lanes = pl.ds(pl.multiple_of(m * span, span), span)
        w = weight[:, lanes]
        c, s = sincos((odd * b) & (NB - 1), NB)
        one = (c[0:1], s[0:1])
        even = rotated((c, s), one)
        turn = (even[0][7:8], even[1][7:8])
        twice = 2.0 * turn[0]
        for parity, start in ((0, (c, s)), (1, even)):
            before = (start[0] * w, start[1] * w)
            now = rotated(before, turn)
            for g in range(8):
                for k in range(2):
                    rows = pl.ds(k * NH + parity * 128 + g * 16, 16)
                    table[rows, lanes] = jnp.concatenate([before[k], now[k]], 0).astype(BF16)
                if g < 7:
                    after = (twice * now[0] - before[0], twice * now[1] - before[1])
                    later = (twice * after[0] - now[0], twice * after[1] - now[1])
                    before, now = after, later


def fill_mix(lags, mix):
    shape = (2 * CH, CH * 2 * L)
    row = lax.broadcasted_iota(jnp.int32, shape, 0)
    col = lax.broadcasted_iota(jnp.int32, shape, 1)
    part_in, chan_in = row >> 4, row & 15
    chan_out, part_out, q = col >> 4, (col >> 3) & 1, col & 7
    here = jnp.where(chan_in == chan_out, 1.0 / math.sqrt(L), 0.0)
    same = part_in == part_out
    sign = jnp.where(part_in == 0, -1.0, 1.0)
    for l in range(L):
        c, s = sincos((lags[l] * q) & (2 * MAXLAG - 1), 2 * MAXLAG)
        rows = pl.ds(l * 2 * CH, 2 * CH)
        mix[0, rows, :] = here * jnp.where(same, c, sign * s)
        mix[1, rows, :] = here * jnp.where(same, -s, sign * c)


def spread_spectra(got, xs, first):
    @pl.loop(0, 4)
    def _(g):
        for e in range(4):
            s = first + g * 4 + e
            xs[2 * s] = got[s, :, 0:128]
            xs[2 * s + 1] = got[s, :, 128:256]


def fold(lags, xs, table, prod_a, prod_b, acc, step_at, count):
    lane = lax.broadcasted_iota(jnp.int32, (CH, 128), 1)

    def products(step, prod):
        first = step * CHUNK
        for l in range(L):
            lag = lags[l]
            whole, rest = lag >> 7, lag & 127
            back = (128 - rest) & 127
            inside = lane < 128 - rest
            moved = None
            for b in range(CHUNK + 1):
                there = xs[first + b + whole]
                ahead = [pltpu.roll(there[k * CH : (k + 1) * CH], back, 1).astype(F32) for k in range(2)]
                if b > 0:
                    here = xs[first + b - 1].astype(F32)
                    re, im = here[0:CH], here[CH : 2 * CH]
                    lre = jnp.where(inside, moved[0], ahead[0])
                    lim = jnp.where(inside, moved[1], ahead[1])
                    lanes = pl.ds((b - 1) * 128, 128)
                    prod[pl.ds(l * 2 * CH, CH), lanes] = (re * lre + im * lim).astype(BF16)
                    prod[pl.ds(l * 2 * CH + CH, CH), lanes] = (im * lre - re * lim).astype(BF16)
                moved = ahead

    def add(step, prod):
        lanes = pl.ds(pl.multiple_of(step * CHUNK * 128, CHUNK * 128), CHUNK * 128)
        acc[...] += lax.dot_general(prod[...], table[:, lanes], NT, preferred_element_type=F32)

    products(step_at(0), prod_a)

    @pl.loop(0, count // 2 - 1)
    def _(i):
        add(step_at(2 * i), prod_a)
        products(step_at(2 * i + 1), prod_b)
        add(step_at(2 * i + 1), prod_b)
        products(step_at(2 * i + 2), prod_a)

    add(step_at(count - 2), prod_a)
    products(step_at(count - 1), prod_b)
    add(step_at(count - 1), prod_b)


def kernel(
    lags, samples, taper, chans, own_bins, out,
    held, tab, ya, yb, spec, got, bins, weight, xs, table, prod_a, prod_b, acc, mix, mine, theirs,
    sem_s, sem_t, bin_send, bin_recv, spec_send, spec_recv, last_send, last_recv,
):
    tm, ch = lax.axis_index("tm"), lax.axis_index("chan")
    me = tm * 16 + ch
    x, core, z, y = tm // 2, tm % 2, ch // 4, ch % 4

    def partner(dx, dc, dz, dy):
        return ((x + dx) % 4) * 2 + (core + dc) % 2, ((z + dz) % 4) * 4 + (y + dy) % 4

    barrier = pltpu.get_barrier_semaphore()

    rows = FR // PARTS
    loads = []
    for p in range(PARTS):
        part = pl.ds(p * rows, rows)
        loads.append(pltpu.make_async_copy(samples.at[:, part], held.at[:, part], sem_s.at[p]))
        loads[-1].start()
    tables = []
    for r in range(RADIX):
        tables.append(pltpu.make_async_copy(chans.at[r], tab.at[r], sem_t.at[r]))
        tables[-1].start()

    @pl.loop(1, NDEV)
    def _(i):
        to = (me + i) % NDEV
        pl.semaphore_signal(barrier, inc=1, device_id=(to // 16, to % 16), device_id_type=MESH)

    for p in range(PARTS):
        loads[p].wait()
        butterflies(held, taper, ya, yb, p)

    for r in range(RADIX):
        tables[r].wait()
        re = lax.dot_general(tab[r], ya[r], NT, preferred_element_type=F32)
        spec[r, :, 0:CH, :] = re.astype(BF16).reshape(GROUP, CH, FR)
        im = lax.dot_general(tab[r], yb[r], NT, preferred_element_type=F32)
        spec[r, :, CH : 2 * CH, :] = im.astype(BF16).reshape(GROUP, CH, FR)

    pl.semaphore_wait(barrier, NDEV - 1)

    bins[pl.ds(pl.multiple_of(tm * 32, 32), 32), :] = own_bins[...]

    @pl.loop(1, 8)
    def _(i):
        pltpu.make_async_remote_copy(
            src_ref=own_bins,
            dst_ref=bins.at[pl.ds(pl.multiple_of(tm * 32, 32), 32)],
            send_sem=bin_send,
            recv_sem=bin_recv,
            device_id=((tm + i) % 8, ch),
            device_id_type=MESH,
        ).start()

    def send_spectra(offset, phase):
        to_tm, to_ch = partner(*offset)
        pltpu.make_async_remote_copy(
            src_ref=spec.at[(y + offset[3]) % 4, to_tm * 4 + to_ch // 4],
            dst_ref=got.at[me],
            send_sem=spec_send,
            recv_sem=spec_recv.at[phase],
            device_id=(to_tm, to_ch),
            device_id_type=MESH,
        ).start()

    for offset in FIRST_ORDER:
        send_spectra(offset, 0)

    got[me] = spec[y, tm * 4 + z]

    fill_mix(lags, mix)

    seven = pltpu.make_async_copy(bins.at[pl.ds(0, 224)], bins.at[pl.ds(0, 224)], bin_recv)
    seven.wait()
    high, low = table.at[pl.ds(0, 32)], table.at[pl.ds(32, 64)]
    def send_second(m):
        n = (m * 13) % 32
        send_spectra((2 * (n % 2), 1, (n // 2) % 4, n // 8), 1)

    def send_last(m):
        late = m // 32
        n = (m * 13) % 32
        send_spectra((1 + 2 * (n % 2), late, (n // 2) % 4, n // 8), 2 + late)

    frame_weights(bins, high, low, weight, send_second)
    fill_table(bins, weight, table, send_last)

    acc[...] = jnp.zeros_like(acc)
    xs[pl.ds(BLK, PADBLK)] = jnp.zeros((PADBLK, 2 * CH, 128), BF16)

    def step_of(at_x, at_core, at_z):
        return (at_x % 4) * 8 + at_core * 4 + at_z

    def first_steps(i):
        return step_of(x + 2 * (i // 7), 0, i % 7)

    def inner(at_core):
        return lambda i: step_of(x + 1 + 2 * (i // 3), at_core, i % 3)

    def third_steps(i):
        late = i // 6
        return (1 - late) * inner(core)(i) + late * step_of(x + core + 2 * (i % 2), 1, 3)

    def fourth_steps(i):
        late, odd = i // 6, i // 8
        end = (1 - odd) * step_of(x + 1 + 2 * (i % 2), 0, 3) + odd * step_of(x + 1 - core + 2 * (i % 2), 1, 3)
        return (1 - late) * inner(1 - core)(i) + late * end

    for phase in range(4):
        shift, at_core = phase // 2, core if phase % 2 == 0 else 1 - core
        came = got.at[pl.ds(0, 31 if phase == 0 else 32)]
        pltpu.make_async_copy(came, came, spec_recv.at[phase]).wait()
        for k in range(2):
            spread_spectra(got, xs, ((x + shift + 2 * k) % 4) * 32 + at_core * 16)
        if phase > 0:
            step_at, count = ((first_steps, 14), (third_steps, 8), (fourth_steps, 10))[phase - 1]
            fold(lags, xs, table, prod_a, prod_b, acc, step_at, count)

    sums = acc[...].T
    exact = dict(preferred_element_type=F32, precision=lax.Precision.HIGHEST)
    res = jnp.dot(sums[0:NH], mix[0], **exact) + jnp.dot(sums[NH:], mix[1], **exact)
    for p in range(2):
        for half in range(2):
            rows = res[p * 128 : (p + 1) * 128, half * 128 : (half + 1) * 128]
            mine[:, 2 * p + half, :] = rows

    for offset in LAST_ORDER:
        to_tm, to_ch = partner(*offset)
        pltpu.make_async_remote_copy(
            src_ref=mine.at[to_tm * 16 + to_ch],
            dst_ref=theirs.at[me],
            send_sem=last_send,
            recv_sem=last_recv,
            device_id=(to_tm, to_ch),
            device_id_type=MESH,
        ).start()
    theirs[me] = mine[me]
    rest = theirs.at[pl.ds(0, NDEV - 1)]
    pltpu.make_async_copy(rest, rest, last_recv).wait()

    for p in range(2):
        for half in range(2):
            turned = theirs[:, 2 * p + half, :].T
            for j in range(CH // 2):
                for ro in range(2):
                    row = j * 16 + ro * 8
                    lanes = pl.ds((half * (CH // 2) + j) * 128, 128)
                    out[ro, p, :, lanes] = turned[row : row + 8]

    sent = bins.at[pl.ds(0, 224)]
    pltpu.make_async_copy(sent, sent, bin_send).wait()
    blocks = got.at[pl.ds(0, NDEV - 1)]
    pltpu.make_async_copy(blocks, blocks, spec_send).wait()
    pltpu.make_async_copy(rest, rest, last_send).wait()


def on_device(samples, window_taper, phase_bins, lag_set):
    return pl.pallas_call(
        kernel,
        out_shape=jax.ShapeDtypeStruct((2, 2, L, K), F32),
        in_specs=[SMEM, ANY, VMEM, ANY, VMEM],
        out_specs=VMEM,
        scratch_shapes=[
            pltpu.VMEM((2, FR, K), F32),
            pltpu.VMEM((RADIX, K // RADIX, 2 * KR), BF16),
            pltpu.VMEM((RADIX, FR, 2 * KR), BF16),
            pltpu.VMEM((RADIX, FR, 2 * KR), BF16),
            pltpu.VMEM((RADIX, GROUP, 2 * CH, FR), BF16),
            pltpu.VMEM((NDEV, 2 * CH, FR), BF16),
            pltpu.VMEM((BLK, 128), jnp.int32),
            pltpu.VMEM((1, T), F32),
            pltpu.VMEM((BLK + PADBLK, 2 * CH, 128), BF16),
            pltpu.VMEM((2 * NH, T), BF16),
            pltpu.VMEM((L * 2 * CH, CHUNK * 128), BF16),
            pltpu.VMEM((L * 2 * CH, CHUNK * 128), BF16),
            pltpu.VMEM((L * 2 * CH, 2 * NH), F32),
            pltpu.VMEM((2, L * 2 * CH, CH * 2 * L), F32),
            pltpu.VMEM((NDEV, 4, 128), F32),
            pltpu.VMEM((NDEV, 4, 128), F32),
            pltpu.SemaphoreType.DMA((PARTS,)),
            pltpu.SemaphoreType.DMA((RADIX,)),
            pltpu.SemaphoreType.DMA,
            pltpu.SemaphoreType.DMA,
            pltpu.SemaphoreType.DMA,
            pltpu.SemaphoreType.DMA((4,)),
            pltpu.SemaphoreType.DMA,
            pltpu.SemaphoreType.DMA,
        ],
        compiler_params=pltpu.CompilerParams(
            vmem_limit_bytes=62 * 2**20, collective_id=0, has_side_effects=True
        ),
        name="cyclic",
    )(lag_set, samples, window_taper.reshape(1, K), jnp.asarray(chan_tables()), phase_bins.reshape(-1, 128))


def solution(mesh):
    placed = (P(None, ("tm", "chan"), None), P(), P("tm"), P())
    return jax.shard_map(
        on_device,
        mesh=mesh,
        in_specs=placed,
        out_specs=P(None, ("tm", "chan"), None, None),
        check_vma=False,
    )
```

```python
import math

import jax
import jax.numpy as jnp
import ml_dtypes
import numpy as np
from jax import lax
from jax.experimental import pallas as pl
from jax.experimental.pallas import tpu as pltpu
from jax.sharding import PartitionSpec as P

K = 2048
NB = 1024
NH = 256
L = 8
MAXLAG = 1024
T = 32768
NDEV = 128
FR = T // NDEV
CH = K // NDEV
RADIX = 4
KR = K // RADIX
GROUP = NDEV // RADIX
BLK = T // 128
PADBLK = 32
CHUNK = 8
STEPS = BLK // CHUNK
PARTS = 4
WIDE = 8
F32 = jnp.float32
BF16 = jnp.bfloat16
NT = (((1,), (1,)), ((), ()))
VMEM = pl.BlockSpec(memory_space=pltpu.VMEM)
SMEM = pl.BlockSpec(memory_space=pltpu.SMEM)
ANY = pl.BlockSpec(memory_space=pl.ANY)
MESH = pl.DeviceIdType.MESH


def hops(offset):
    return sum((0, 1, 2, 1)[offset[axis]] for axis in (0, 2, 3))


def offsets():
    mixed = [(n % 4, n // 64, (n // 4) % 4, (n // 16) % 4) for n in (i * 37 % NDEV for i in range(1, NDEV))]
    return sorted(mixed, key=lambda offset: -hops(offset))


def phase_of(offset):
    return 2 * (offset[0] % 2) + offset[1]


LAST_ORDER = offsets()
FIRST_ORDER = [offset for offset in LAST_ORDER if phase_of(offset) == 0]


def chan_tables():
    r = np.arange(RADIX)[:, None, None]
    i = np.arange(GROUP)[None, :, None]
    j = np.arange(CH)[None, None, :]
    chan = (NDEV * j + RADIX * i + r).reshape(-1)
    angle = (chan[:, None] * np.arange(KR)[None, :] % K) * (2.0 * math.pi / K)
    both = np.concatenate([np.cos(angle), np.sin(angle)], 1).astype(np.float32) * np.float32(1.0 / math.sqrt(K))
    return both.astype(ml_dtypes.bfloat16).reshape(RADIX, K // RADIX, 2 * KR)


def butterflies(held, taper, ya, yb, part):
    rows = FR // PARTS

    @pl.loop(0, rows // 16)
    def _(g):
        at = pl.ds(pl.multiple_of(part * rows + g * 16, 16), 16)
        for b in range(KR // 128):
            x = []
            for m in range(RADIX):
                lanes = pl.ds(m * KR + b * 128, 128)
                w = taper[:, lanes]
                x.append([(held[c, at, lanes] * w).astype(BF16).astype(F32) for c in range(2)])
            er, ei = x[0][0] + x[2][0], x[0][1] + x[2][1]
            fr, fi = x[1][0] + x[3][0], x[1][1] + x[3][1]
            gr, gi = x[0][0] - x[2][0], x[0][1] - x[2][1]
            hr, hi = x[1][0] - x[3][0], x[1][1] - x[3][1]
            y = [(er + fr, ei + fi), (gr + hi, gi - hr), (er - fr, ei - fi), (gr - hi, gi + hr)]
            for r in range(RADIX):
                re, im = y[r][0].astype(BF16), y[r][1].astype(BF16)
                ya[r, at, pl.ds(b * 128, 128)] = re
                ya[r, at, pl.ds(KR + b * 128, 128)] = im
                yb[r, at, pl.ds(b * 128, 128)] = im
                yb[r, at, pl.ds(KR + b * 128, 128)] = -re


def sincos(m, period):
    x = (m - period // 2).astype(F32) * (math.pi / period)
    z = x * x
    s = x * (1.0 + z * (-1.0 / 6 + z * (1.0 / 120 + z * (-1.0 / 5040 + z * (1.0 / 362880 - z / 39916800)))))
    c = 1.0 + z * (-0.5 + z * (1.0 / 24 + z * (-1.0 / 720 + z * (1.0 / 40320 + z * (-1.0 / 3628800 + z / 479001600)))))
    return 2.0 * s * s - 1.0, -2.0 * s * c


def rotated(e, f):
    return e[0] * f[0] - e[1] * f[1], e[0] * f[1] + e[1] * f[0]


def bins_of(bins, first, count):
    return jnp.concatenate([bins[pl.ds(first + i, 1), :] for i in range(count)], 1)


def frame_weights(bins, high, low, weight, beside):
    span = 8 * 128
    row32 = lax.broadcasted_iota(jnp.int32, (32, span), 0)

    @pl.loop(0, BLK // 8)
    def _(m):
        beside(m)
        b = bins_of(bins, m * 8, 8)
        lanes = pl.ds(pl.multiple_of(m * span, span), span)
        high[:, lanes] = ((b >> 5) == row32).astype(F32).astype(BF16)
        ones = ((b & 31) == row32).astype(F32).astype(BF16)
        low[0:32, lanes] = ones
        low[32:64, lanes] = ones

    part = 4096
    hist = jnp.zeros((32, 32), F32)
    for p in range(T // part):
        lanes = pl.ds(p * part, part)
        hist = hist + lax.dot_general(high[:, lanes], low[0:32, lanes], NT, preferred_element_type=F32)
    inverse = (1.0 / math.sqrt(NB)) / jnp.maximum(hist, 1.0)
    first = inverse.astype(BF16)
    second = (inverse - first.astype(F32)).astype(BF16)
    both = jnp.concatenate([first, second], 1)

    for p in range(T // part):
        lanes = pl.ds(p * part, part)
        rows = jnp.dot(both, low[:, lanes], preferred_element_type=F32)
        weight[:, lanes] = jnp.sum(rows * high[:, lanes].astype(F32), axis=0, keepdims=True)


def fill_table(bins, weight, table, beside):
    span = WIDE * 128
    odd = 2 * lax.broadcasted_iota(jnp.int32, (8, span), 0) + 1

    @pl.loop(0, BLK // WIDE)
    def _(m):
        beside(m)
        b = bins_of(bins, m * WIDE, WIDE)
        lanes = pl.ds(pl.multiple_of(m * span, span), span)
        w = weight[:, lanes]
        c, s = sincos((odd * b) & (NB - 1), NB)
        one = (c[0:1], s[0:1])
        even = rotated((c, s), one)
        turn = (even[0][7:8], even[1][7:8])
        twice = 2.0 * turn[0]
        for parity, start in ((0, (c, s)), (1, even)):
            before = (start[0] * w, start[1] * w)
            now = rotated(before, turn)
            for g in range(8):
                for k in range(2):
                    rows = pl.ds(k * NH + parity * 128 + g * 16, 16)
                    table[rows, lanes] = jnp.concatenate([before[k], now[k]], 0).astype(BF16)
                if g < 7:
                    after = (twice * now[0] - before[0], twice * now[1] - before[1])
                    later = (twice * after[0] - now[0], twice * after[1] - now[1])
                    before, now = after, later


def fill_mix(lags, mix):
    shape = (2 * CH, CH * 2 * L)
    row = lax.broadcasted_iota(jnp.int32, shape, 0)
    col = lax.broadcasted_iota(jnp.int32, shape, 1)
    part_in, chan_in = row >> 4, row & 15
    chan_out, part_out, q = col >> 4, (col >> 3) & 1, col & 7
    here = jnp.where(chan_in == chan_out, 1.0 / math.sqrt(L), 0.0)
    same = part_in == part_out
    sign = jnp.where(part_in == 0, -1.0, 1.0)
    for l in range(L):
        c, s = sincos((lags[l] * q) & (2 * MAXLAG - 1), 2 * MAXLAG)
        rows = pl.ds(l * 2 * CH, 2 * CH)
        mix[0, rows, :] = here * jnp.where(same, c, sign * s)
        mix[1, rows, :] = here * jnp.where(same, -s, sign * c)


def spread_spectra(got, xs, first):
    @pl.loop(0, 4)
    def _(g):
        for e in range(4):
            s = first + g * 4 + e
            xs[2 * s] = got[s, :, 0:128]
            xs[2 * s + 1] = got[s, :, 128:256]


def fold(lags, xs, table, prod_a, prod_b, acc, step_at, count):
    lane = lax.broadcasted_iota(jnp.int32, (CH, 128), 1)

    def products(step, prod):
        first = step * CHUNK
        for l in range(L):
            lag = lags[l]
            whole, rest = lag >> 7, lag & 127
            back = (128 - rest) & 127
            inside = lane < 128 - rest
            moved = None
            for b in range(CHUNK + 1):
                there = xs[first + b + whole]
                ahead = [pltpu.roll(there[k * CH : (k + 1) * CH], back, 1) for k in range(2)]
                if b > 0:
                    here = xs[first + b - 1]
                    re, im = here[0:CH], here[CH : 2 * CH]
                    lre = jnp.where(inside, moved[0], ahead[0])
                    lim = jnp.where(inside, moved[1], ahead[1])
                    lanes = pl.ds((b - 1) * 128, 128)
                    prod[pl.ds(l * 2 * CH, CH), lanes] = re * lre + im * lim
                    prod[pl.ds(l * 2 * CH + CH, CH), lanes] = im * lre - re * lim
                moved = ahead

    def add(step, prod):
        lanes = pl.ds(pl.multiple_of(step * CHUNK * 128, CHUNK * 128), CHUNK * 128)
        acc[...] += lax.dot_general(prod[...], table[:, lanes], NT, preferred_element_type=F32)

    products(step_at(0), prod_a)

    @pl.loop(0, count // 2 - 1)
    def _(i):
        add(step_at(2 * i), prod_a)
        products(step_at(2 * i + 1), prod_b)
        add(step_at(2 * i + 1), prod_b)
        products(step_at(2 * i + 2), prod_a)

    add(step_at(count - 2), prod_a)
    products(step_at(count - 1), prod_b)
    add(step_at(count - 1), prod_b)


def kernel(
    lags, samples, taper, chans, own_bins, out,
    held, tab, ya, yb, spec, got, bins, weight, xs, table, prod_a, prod_b, acc, mix, mine, theirs,
    sem_s, sem_t, bin_send, bin_recv, spec_send, spec_recv, last_send, last_recv,
):
    tm, ch = lax.axis_index("tm"), lax.axis_index("chan")
    me = tm * 16 + ch
    x, core, z, y = tm // 2, tm % 2, ch // 4, ch % 4

    def partner(dx, dc, dz, dy):
        return ((x + dx) % 4) * 2 + (core + dc) % 2, ((z + dz) % 4) * 4 + (y + dy) % 4

    barrier = pltpu.get_barrier_semaphore()

    rows = FR // PARTS
    loads = []
    for p in range(PARTS):
        part = pl.ds(p * rows, rows)
        loads.append(pltpu.make_async_copy(samples.at[:, part], held.at[:, part], sem_s.at[p]))
        loads[-1].start()
    tables = []
    for r in range(RADIX):
        tables.append(pltpu.make_async_copy(chans.at[r], tab.at[r], sem_t.at[r]))
        tables[-1].start()

    for offset in LAST_ORDER:
        pl.semaphore_signal(barrier, inc=1, device_id=partner(*offset), device_id_type=MESH)

    for p in range(PARTS):
        loads[p].wait()
        butterflies(held, taper, ya, yb, p)

    for r in range(RADIX):
        tables[r].wait()
        re = lax.dot_general(tab[r], ya[r], NT, preferred_element_type=F32)
        spec[r, :, 0:CH, :] = re.astype(BF16).reshape(GROUP, CH, FR)
        im = lax.dot_general(tab[r], yb[r], NT, preferred_element_type=F32)
        spec[r, :, CH : 2 * CH, :] = im.astype(BF16).reshape(GROUP, CH, FR)

    pl.semaphore_wait(barrier, NDEV - 1)

    bins[pl.ds(pl.multiple_of(tm * 32, 32), 32), :] = own_bins[...]

    @pl.loop(1, 8)
    def _(i):
        pltpu.make_async_remote_copy(
            src_ref=own_bins,
            dst_ref=bins.at[pl.ds(pl.multiple_of(tm * 32, 32), 32)],
            send_sem=bin_send,
            recv_sem=bin_recv,
            device_id=((tm + i) % 8, ch),
            device_id_type=MESH,
        ).start()

    def send_spectra(offset, phase):
        to_tm, to_ch = partner(*offset)
        pltpu.make_async_remote_copy(
            src_ref=spec.at[(y + offset[3]) % 4, to_tm * 4 + to_ch // 4],
            dst_ref=got.at[me],
            send_sem=spec_send,
            recv_sem=spec_recv.at[phase],
            device_id=(to_tm, to_ch),
            device_id_type=MESH,
        ).start()

    for offset in FIRST_ORDER:
        send_spectra(offset, 0)

    got[me] = spec[y, tm * 4 + z]

    fill_mix(lags, mix)

    seven = pltpu.make_async_copy(bins.at[pl.ds(0, 224)], bins.at[pl.ds(0, 224)], bin_recv)
    seven.wait()
    high, low = table.at[pl.ds(0, 32)], table.at[pl.ds(32, 64)]
    def send_second(m):
        n = (m * 13) % 32
        send_spectra((2 * (n % 2), 1, (n // 2) % 4, n // 8), 1)

    def send_last(m):
        for k in range(2):
            late = m // 16
            n = ((2 * m + k) * 13) % 32
            send_spectra((1 + 2 * (n % 2), late, (n // 2) % 4, n // 8), 2 + late)

    frame_weights(bins, high, low, weight, send_second)
    fill_table(bins, weight, table, send_last)

    acc[...] = jnp.zeros_like(acc)
    xs[pl.ds(BLK, PADBLK)] = jnp.zeros((PADBLK, 2 * CH, 128), BF16)

    def step_of(at_x, at_core, at_z):
        return (at_x % 4) * 8 + at_core * 4 + at_z

    def first_steps(i):
        return step_of(x + 2 * (i // 7), 0, i % 7)

    def inner(at_core):
        return lambda i: step_of(x + 1 + 2 * (i // 3), at_core, i % 3)

    def third_steps(i):
        late = i // 6
        return (1 - late) * inner(core)(i) + late * step_of(x + core + 2 * (i % 2), 1, 3)

    def fourth_steps(i):
        late, odd = i // 6, i // 8
        end = (1 - odd) * step_of(x + 1 + 2 * (i % 2), 0, 3) + odd * step_of(x + 1 - core + 2 * (i % 2), 1, 3)
        return (1 - late) * inner(1 - core)(i) + late * end

    for phase in range(4):
        shift, at_core = phase // 2, core if phase % 2 == 0 else 1 - core
        came = got.at[pl.ds(0, 31 if phase == 0 else 32)]
        pltpu.make_async_copy(came, came, spec_recv.at[phase]).wait()
        for k in range(2):
            spread_spectra(got, xs, ((x + shift + 2 * k) % 4) * 32 + at_core * 16)
        if phase > 0:
            step_at, count = ((first_steps, 14), (third_steps, 8), (fourth_steps, 10))[phase - 1]
            fold(lags, xs, table, prod_a, prod_b, acc, step_at, count)

    sums = acc[...].T
    exact = dict(preferred_element_type=F32, precision=lax.Precision.HIGHEST)
    res = jnp.dot(sums[0:NH], mix[0], **exact) + jnp.dot(sums[NH:], mix[1], **exact)
    for p in range(2):
        for half in range(2):
            rows = res[p * 128 : (p + 1) * 128, half * 128 : (half + 1) * 128]
            mine[:, 2 * p + half, :] = rows

    for offset in LAST_ORDER:
        to_tm, to_ch = partner(*offset)
        pltpu.make_async_remote_copy(
            src_ref=mine.at[to_tm * 16 + to_ch],
            dst_ref=theirs.at[me],
            send_sem=last_send,
            recv_sem=last_recv,
            device_id=(to_tm, to_ch),
            device_id_type=MESH,
        ).start()
    theirs[me] = mine[me]
    rest = theirs.at[pl.ds(0, NDEV - 1)]
    pltpu.make_async_copy(rest, rest, last_recv).wait()

    for p in range(2):
        for half in range(2):
            turned = theirs[:, 2 * p + half, :].T
            for j in range(CH // 2):
                for ro in range(2):
                    row = j * 16 + ro * 8
                    lanes = pl.ds((half * (CH // 2) + j) * 128, 128)
                    out[ro, p, :, lanes] = turned[row : row + 8]

    sent = bins.at[pl.ds(0, 224)]
    pltpu.make_async_copy(sent, sent, bin_send).wait()
    blocks = got.at[pl.ds(0, NDEV - 1)]
    pltpu.make_async_copy(blocks, blocks, spec_send).wait()
    pltpu.make_async_copy(rest, rest, last_send).wait()


def on_device(samples, window_taper, phase_bins, lag_set):
    return pl.pallas_call(
        kernel,
        out_shape=jax.ShapeDtypeStruct((2, 2, L, K), F32),
        in_specs=[SMEM, ANY, VMEM, ANY, VMEM],
        out_specs=VMEM,
        scratch_shapes=[
            pltpu.VMEM((2, FR, K), F32),
            pltpu.VMEM((RADIX, K // RADIX, 2 * KR), BF16),
            pltpu.VMEM((RADIX, FR, 2 * KR), BF16),
            pltpu.VMEM((RADIX, FR, 2 * KR), BF16),
            pltpu.VMEM((RADIX, GROUP, 2 * CH, FR), BF16),
            pltpu.VMEM((NDEV, 2 * CH, FR), BF16),
            pltpu.VMEM((BLK, 128), jnp.int32),
            pltpu.VMEM((1, T), F32),
            pltpu.VMEM((BLK + PADBLK, 2 * CH, 128), BF16),
            pltpu.VMEM((2 * NH, T), BF16),
            pltpu.VMEM((L * 2 * CH, CHUNK * 128), BF16),
            pltpu.VMEM((L * 2 * CH, CHUNK * 128), BF16),
            pltpu.VMEM((L * 2 * CH, 2 * NH), F32),
            pltpu.VMEM((2, L * 2 * CH, CH * 2 * L), F32),
            pltpu.VMEM((NDEV, 4, 128), F32),
            pltpu.VMEM((NDEV, 4, 128), F32),
            pltpu.SemaphoreType.DMA((PARTS,)),
            pltpu.SemaphoreType.DMA((RADIX,)),
            pltpu.SemaphoreType.DMA,
            pltpu.SemaphoreType.DMA,
            pltpu.SemaphoreType.DMA,
            pltpu.SemaphoreType.DMA((4,)),
            pltpu.SemaphoreType.DMA,
            pltpu.SemaphoreType.DMA,
        ],
        compiler_params=pltpu.CompilerParams(
            vmem_limit_bytes=62 * 2**20, collective_id=0, has_side_effects=True
        ),
        name="cyclic",
    )(lag_set, samples, window_taper.reshape(1, K), jnp.asarray(chan_tables()), phase_bins.reshape(-1, 128))


def solution(mesh):
    placed = (P(None, ("tm", "chan"), None), P(), P("tm"), P())
    return jax.shard_map(
        on_device,
        mesh=mesh,
        in_specs=placed,
        out_specs=P(None, ("tm", "chan"), None, None),
        check_vma=False,
    )
```

```python
import math

import jax
import jax.numpy as jnp
import ml_dtypes
import numpy as np
from jax import lax
from jax.experimental import pallas as pl
from jax.experimental.pallas import tpu as pltpu
from jax.sharding import PartitionSpec as P

K = 2048
NB = 1024
NH = 256
L = 8
MAXLAG = 1024
T = 32768
NDEV = 128
FR = T // NDEV
CH = K // NDEV
RADIX = 4
KR = K // RADIX
GROUP = NDEV // RADIX
BLK = T // 128
PADBLK = 32
CHUNK = 8
STEPS = BLK // CHUNK
PARTS = 4
WIDE = 8
F32 = jnp.float32
BF16 = jnp.bfloat16
NT = (((1,), (1,)), ((), ()))
VMEM = pl.BlockSpec(memory_space=pltpu.VMEM)
SMEM = pl.BlockSpec(memory_space=pltpu.SMEM)
ANY = pl.BlockSpec(memory_space=pl.ANY)
MESH = pl.DeviceIdType.MESH


def hops(offset):
    return sum((0, 1, 2, 1)[offset[axis]] for axis in (0, 2, 3))


def offsets():
    mixed = [(n % 4, n // 64, (n // 4) % 4, (n // 16) % 4) for n in (i * 37 % NDEV for i in range(1, NDEV))]
    return sorted(mixed, key=lambda offset: -hops(offset))


def phase_of(offset):
    return 2 * (offset[0] % 2) + offset[1]


LAST_ORDER = offsets()
FIRST_ORDER = [offset for offset in LAST_ORDER if phase_of(offset) == 0]


def chan_tables():
    r = np.arange(RADIX)[:, None, None]
    i = np.arange(GROUP)[None, :, None]
    j = np.arange(CH)[None, None, :]
    chan = (NDEV * j + RADIX * i + r).reshape(-1)
    angle = (chan[:, None] * np.arange(KR)[None, :] % K) * (2.0 * math.pi / K)
    both = np.concatenate([np.cos(angle), np.sin(angle)], 1).astype(np.float32) * np.float32(1.0 / math.sqrt(K))
    return both.astype(ml_dtypes.bfloat16).reshape(RADIX, K // RADIX, 2 * KR)


def butterflies(held, taper, ya, yb, part):
    rows = FR // PARTS

    @pl.loop(0, rows // 16)
    def _(g):
        at = pl.ds(pl.multiple_of(part * rows + g * 16, 16), 16)
        for b in range(KR // 128):
            x = []
            for m in range(RADIX):
                lanes = pl.ds(m * KR + b * 128, 128)
                w = taper[:, lanes]
                x.append([(held[c, at, lanes] * w).astype(BF16).astype(F32) for c in range(2)])
            er, ei = x[0][0] + x[2][0], x[0][1] + x[2][1]
            fr, fi = x[1][0] + x[3][0], x[1][1] + x[3][1]
            gr, gi = x[0][0] - x[2][0], x[0][1] - x[2][1]
            hr, hi = x[1][0] - x[3][0], x[1][1] - x[3][1]
            y = [(er + fr, ei + fi), (gr + hi, gi - hr), (er - fr, ei - fi), (gr - hi, gi + hr)]
            for r in range(RADIX):
                re, im = y[r][0].astype(BF16), y[r][1].astype(BF16)
                ya[r, at, pl.ds(b * 128, 128)] = re
                ya[r, at, pl.ds(KR + b * 128, 128)] = im
                yb[r, at, pl.ds(b * 128, 128)] = im
                yb[r, at, pl.ds(KR + b * 128, 128)] = -re


def sincos(m, period):
    x = (m - period // 2).astype(F32) * (math.pi / period)
    z = x * x
    s = x * (1.0 + z * (-1.0 / 6 + z * (1.0 / 120 + z * (-1.0 / 5040 + z * (1.0 / 362880 - z / 39916800)))))
    c = 1.0 + z * (-0.5 + z * (1.0 / 24 + z * (-1.0 / 720 + z * (1.0 / 40320 + z * (-1.0 / 3628800 + z / 479001600)))))
    return 2.0 * s * s - 1.0, -2.0 * s * c


def rotated(e, f):
    return e[0] * f[0] - e[1] * f[1], e[0] * f[1] + e[1] * f[0]


def bins_of(bins, first, count):
    return jnp.concatenate([bins[pl.ds(first + i, 1), :] for i in range(count)], 1)


def frame_weights(bins, high, low, weight, beside):
    span = 8 * 128
    row32 = lax.broadcasted_iota(jnp.int32, (32, span), 0)

    @pl.loop(0, BLK // 8)
    def _(m):
        beside(m)
        b = bins_of(bins, m * 8, 8)
        lanes = pl.ds(pl.multiple_of(m * span, span), span)
        high[:, lanes] = ((b >> 5) == row32).astype(F32).astype(BF16)
        ones = ((b & 31) == row32).astype(F32).astype(BF16)
        low[0:32, lanes] = ones
        low[32:64, lanes] = ones

    part = 4096
    hist = jnp.zeros((32, 32), F32)
    for p in range(T // part):
        lanes = pl.ds(p * part, part)
        hist = hist + lax.dot_general(high[:, lanes], low[0:32, lanes], NT, preferred_element_type=F32)
    inverse = (1.0 / math.sqrt(NB)) / jnp.maximum(hist, 1.0)
    first = inverse.astype(BF16)
    second = (inverse - first.astype(F32)).astype(BF16)
    both = jnp.concatenate([first, second], 1)

    for p in range(T // part):
        lanes = pl.ds(p * part, part)
        rows = jnp.dot(both, low[:, lanes], preferred_element_type=F32)
        weight[:, lanes] = jnp.sum(rows * high[:, lanes].astype(F32), axis=0, keepdims=True)


def fill_table(bins, weight, table, beside):
    span = WIDE * 128
    odd = 2 * lax.broadcasted_iota(jnp.int32, (8, span), 0) + 1

    @pl.loop(0, BLK // WIDE)
    def _(m):
        beside(m)
        b = bins_of(bins, m * WIDE, WIDE)
        lanes = pl.ds(pl.multiple_of(m * span, span), span)
        w = weight[:, lanes]
        c, s = sincos((odd * b) & (NB - 1), NB)
        one = (c[0:1], s[0:1])
        even = rotated((c, s), one)
        turn = (even[0][7:8], even[1][7:8])
        twice = 2.0 * turn[0]
        for parity, start in ((0, (c, s)), (1, even)):
            before = (start[0] * w, start[1] * w)
            now = rotated(before, turn)
            for g in range(8):
                for k in range(2):
                    rows = pl.ds(k * NH + parity * 128 + g * 16, 16)
                    table[rows, lanes] = jnp.concatenate([before[k], now[k]], 0).astype(BF16)
                if g < 7:
                    after = (twice * now[0] - before[0], twice * now[1] - before[1])
                    later = (twice * after[0] - now[0], twice * after[1] - now[1])
                    before, now = after, later


def fill_mix(lags, mix):
    shape = (2 * CH, CH * 2 * L)
    row = lax.broadcasted_iota(jnp.int32, shape, 0)
    col = lax.broadcasted_iota(jnp.int32, shape, 1)
    part_in, chan_in = row >> 4, row & 15
    chan_out, part_out, q = col >> 4, (col >> 3) & 1, col & 7
    here = jnp.where(chan_in == chan_out, 1.0 / math.sqrt(L), 0.0)
    same = part_in == part_out
    sign = jnp.where(part_in == 0, -1.0, 1.0)
    for l in range(L):
        c, s = sincos((lags[l] * q) & (2 * MAXLAG - 1), 2 * MAXLAG)
        rows = pl.ds(l * 2 * CH, 2 * CH)
        mix[0, rows, :] = here * jnp.where(same, c, sign * s)
        mix[1, rows, :] = here * jnp.where(same, -s, sign * c)


def spread_spectra(got, xs, first):
    @pl.loop(0, 4)
    def _(g):
        for e in range(4):
            s = first + g * 4 + e
            xs[2 * s] = got[s, :, 0:128]
            xs[2 * s + 1] = got[s, :, 128:256]


def fold(lags, xs, table, prod_a, prod_b, acc, step_at, count):
    lane = lax.broadcasted_iota(jnp.int32, (CH, 128), 1)

    def products(step, prod):
        first = step * CHUNK
        for l in range(L):
            lag = lags[l]
            whole, rest = lag >> 7, lag & 127
            back = (128 - rest) & 127
            inside = lane < 128 - rest
            moved = None
            for b in range(CHUNK + 1):
                there = xs[first + b + whole]
                ahead = [pltpu.roll(there[k * CH : (k + 1) * CH], back, 1) for k in range(2)]
                if b > 0:
                    here = xs[first + b - 1]
                    re, im = here[0:CH], here[CH : 2 * CH]
                    lre = jnp.where(inside, moved[0], ahead[0])
                    lim = jnp.where(inside, moved[1], ahead[1])
                    lanes = pl.ds((b - 1) * 128, 128)
                    prod[pl.ds(l * 2 * CH, CH), lanes] = re * lre + im * lim
                    prod[pl.ds(l * 2 * CH + CH, CH), lanes] = im * lre - re * lim
                moved = ahead

    def add(step, prod):
        lanes = pl.ds(pl.multiple_of(step * CHUNK * 128, CHUNK * 128), CHUNK * 128)
        acc[...] += lax.dot_general(prod[...], table[:, lanes], NT, preferred_element_type=F32)

    products(step_at(0), prod_a)

    @pl.loop(0, count // 2 - 1)
    def _(i):
        add(step_at(2 * i), prod_a)
        products(step_at(2 * i + 1), prod_b)
        add(step_at(2 * i + 1), prod_b)
        products(step_at(2 * i + 2), prod_a)

    add(step_at(count - 2), prod_a)
    products(step_at(count - 1), prod_b)
    add(step_at(count - 1), prod_b)


def kernel(
    lags, samples, taper, chans, own_bins, out,
    held, tab, ya, yb, spec, got, bins, weight, xs, table, prod_a, prod_b, acc, mix, mine, theirs,
    sem_s, sem_t, bin_send, bin_recv, spec_send, spec_recv, last_send, last_recv,
):
    tm, ch = lax.axis_index("tm"), lax.axis_index("chan")
    me = tm * 16 + ch
    x, core, z, y = tm // 2, tm % 2, ch // 4, ch % 4

    def partner(dx, dc, dz, dy):
        return ((x + dx) % 4) * 2 + (core + dc) % 2, ((z + dz) % 4) * 4 + (y + dy) % 4

    barrier = pltpu.get_barrier_semaphore()

    rows = FR // PARTS
    loads = []
    for p in range(PARTS):
        part = pl.ds(p * rows, rows)
        loads.append(pltpu.make_async_copy(samples.at[:, part], held.at[:, part], sem_s.at[p]))
        loads[-1].start()
    tables = []
    for r in range(RADIX):
        tables.append(pltpu.make_async_copy(chans.at[r], tab.at[r], sem_t.at[r]))
        tables[-1].start()

    for offset in LAST_ORDER:
        pl.semaphore_signal(barrier, inc=1, device_id=partner(*offset), device_id_type=MESH)

    for p in range(PARTS):
        loads[p].wait()
        butterflies(held, taper, ya, yb, p)

    for r in range(RADIX):
        tables[r].wait()
        re = lax.dot_general(tab[r], ya[r], NT, preferred_element_type=F32)
        spec[r, :, 0:CH, :] = re.astype(BF16).reshape(GROUP, CH, FR)
        im = lax.dot_general(tab[r], yb[r], NT, preferred_element_type=F32)
        spec[r, :, CH : 2 * CH, :] = im.astype(BF16).reshape(GROUP, CH, FR)

    pl.semaphore_wait(barrier, NDEV - 1)

    bins[pl.ds(pl.multiple_of(tm * 32, 32), 32), :] = own_bins[...]

    @pl.loop(1, 8)
    def _(i):
        pltpu.make_async_remote_copy(
            src_ref=own_bins,
            dst_ref=bins.at[pl.ds(pl.multiple_of(tm * 32, 32), 32)],
            send_sem=bin_send,
            recv_sem=bin_recv,
            device_id=((tm + i) % 8, ch),
            device_id_type=MESH,
        ).start()

    def send_spectra(offset, phase):
        to_tm, to_ch = partner(*offset)
        pltpu.make_async_remote_copy(
            src_ref=spec.at[(y + offset[3]) % 4, to_tm * 4 + to_ch // 4],
            dst_ref=got.at[me],
            send_sem=spec_send,
            recv_sem=spec_recv.at[phase],
            device_id=(to_tm, to_ch),
            device_id_type=MESH,
        ).start()

    for offset in FIRST_ORDER:
        send_spectra(offset, 0)

    got[me] = spec[y, tm * 4 + z]

    fill_mix(lags, mix)

    seven = pltpu.make_async_copy(bins.at[pl.ds(0, 224)], bins.at[pl.ds(0, 224)], bin_recv)
    seven.wait()
    high, low = table.at[pl.ds(0, 32)], table.at[pl.ds(32, 64)]
    def send_second(m):
        for k in range(2):
            late = m // 16
            n = ((2 * m + k) * 13) % 32
            send_spectra((late + 2 * (n % 2), 1 - late, (n // 2) % 4, n // 8), 1 + late)

    def send_last(m):
        n = (m * 13) % 32
        send_spectra((1 + 2 * (n % 2), 1, (n // 2) % 4, n // 8), 3)

    frame_weights(bins, high, low, weight, send_second)
    fill_table(bins, weight, table, send_last)

    acc[...] = jnp.zeros_like(acc)
    xs[pl.ds(BLK, PADBLK)] = jnp.zeros((PADBLK, 2 * CH, 128), BF16)

    def step_of(at_x, at_core, at_z):
        return (at_x % 4) * 8 + at_core * 4 + at_z

    def first_steps(i):
        return step_of(x + 2 * (i // 7), 0, i % 7)

    def inner(at_core):
        return lambda i: step_of(x + 1 + 2 * (i // 3), at_core, i % 3)

    def third_steps(i):
        late = i // 6
        return (1 - late) * inner(core)(i) + late * step_of(x + core + 2 * (i % 2), 1, 3)

    def fourth_steps(i):
        late, odd = i // 6, i // 8
        end = (1 - odd) * step_of(x + 1 + 2 * (i % 2), 0, 3) + odd * step_of(x + 1 - core + 2 * (i % 2), 1, 3)
        return (1 - late) * inner(1 - core)(i) + late * end

    for phase in range(4):
        shift, at_core = phase // 2, core if phase % 2 == 0 else 1 - core
        came = got.at[pl.ds(0, 31 if phase == 0 else 32)]
        pltpu.make_async_copy(came, came, spec_recv.at[phase]).wait()
        for k in range(2):
            spread_spectra(got, xs, ((x + shift + 2 * k) % 4) * 32 + at_core * 16)
        if phase > 0:
            step_at, count = ((first_steps, 14), (third_steps, 8), (fourth_steps, 10))[phase - 1]
            fold(lags, xs, table, prod_a, prod_b, acc, step_at, count)

    sums = acc[...].T
    exact = dict(preferred_element_type=F32, precision=lax.Precision.HIGHEST)
    res = jnp.dot(sums[0:NH], mix[0], **exact) + jnp.dot(sums[NH:], mix[1], **exact)
    for p in range(2):
        for half in range(2):
            rows = res[p * 128 : (p + 1) * 128, half * 128 : (half + 1) * 128]
            mine[:, 2 * p + half, :] = rows

    for offset in LAST_ORDER:
        to_tm, to_ch = partner(*offset)
        pltpu.make_async_remote_copy(
            src_ref=mine.at[to_tm * 16 + to_ch],
            dst_ref=theirs.at[me],
            send_sem=last_send,
            recv_sem=last_recv,
            device_id=(to_tm, to_ch),
            device_id_type=MESH,
        ).start()
    theirs[me] = mine[me]
    rest = theirs.at[pl.ds(0, NDEV - 1)]
    pltpu.make_async_copy(rest, rest, last_recv).wait()

    for p in range(2):
        for half in range(2):
            turned = theirs[:, 2 * p + half, :].T
            for j in range(CH // 2):
                for ro in range(2):
                    row = j * 16 + ro * 8
                    lanes = pl.ds((half * (CH // 2) + j) * 128, 128)
                    out[ro, p, :, lanes] = turned[row : row + 8]

    sent = bins.at[pl.ds(0, 224)]
    pltpu.make_async_copy(sent, sent, bin_send).wait()
    blocks = got.at[pl.ds(0, NDEV - 1)]
    pltpu.make_async_copy(blocks, blocks, spec_send).wait()
    pltpu.make_async_copy(rest, rest, last_send).wait()


def on_device(samples, window_taper, phase_bins, lag_set):
    return pl.pallas_call(
        kernel,
        out_shape=jax.ShapeDtypeStruct((2, 2, L, K), F32),
        in_specs=[SMEM, ANY, VMEM, ANY, VMEM],
        out_specs=VMEM,
        scratch_shapes=[
            pltpu.VMEM((2, FR, K), F32),
            pltpu.VMEM((RADIX, K // RADIX, 2 * KR), BF16),
            pltpu.VMEM((RADIX, FR, 2 * KR), BF16),
            pltpu.VMEM((RADIX, FR, 2 * KR), BF16),
            pltpu.VMEM((RADIX, GROUP, 2 * CH, FR), BF16),
            pltpu.VMEM((NDEV, 2 * CH, FR), BF16),
            pltpu.VMEM((BLK, 128), jnp.int32),
            pltpu.VMEM((1, T), F32),
            pltpu.VMEM((BLK + PADBLK, 2 * CH, 128), BF16),
            pltpu.VMEM((2 * NH, T), BF16),
            pltpu.VMEM((L * 2 * CH, CHUNK * 128), BF16),
            pltpu.VMEM((L * 2 * CH, CHUNK * 128), BF16),
            pltpu.VMEM((L * 2 * CH, 2 * NH), F32),
            pltpu.VMEM((2, L * 2 * CH, CH * 2 * L), F32),
            pltpu.VMEM((NDEV, 4, 128), F32),
            pltpu.VMEM((NDEV, 4, 128), F32),
            pltpu.SemaphoreType.DMA((PARTS,)),
            pltpu.SemaphoreType.DMA((RADIX,)),
            pltpu.SemaphoreType.DMA,
            pltpu.SemaphoreType.DMA,
            pltpu.SemaphoreType.DMA,
            pltpu.SemaphoreType.DMA((4,)),
            pltpu.SemaphoreType.DMA,
            pltpu.SemaphoreType.DMA,
        ],
        compiler_params=pltpu.CompilerParams(
            vmem_limit_bytes=62 * 2**20, collective_id=0, has_side_effects=True
        ),
        name="cyclic",
    )(lag_set, samples, window_taper.reshape(1, K), jnp.asarray(chan_tables()), phase_bins.reshape(-1, 128))


def solution(mesh):
    placed = (P(None, ("tm", "chan"), None), P(), P("tm"), P())
    return jax.shard_map(
        on_device,
        mesh=mesh,
        in_specs=placed,
        out_specs=P(None, ("tm", "chan"), None, None),
        check_vma=False,
    )
```

```python
import math

import jax
import jax.numpy as jnp
import ml_dtypes
import numpy as np
from jax import lax
from jax.experimental import pallas as pl
from jax.experimental.pallas import tpu as pltpu
from jax.sharding import PartitionSpec as P

K = 2048
NB = 1024
NH = 256
L = 8
MAXLAG = 1024
T = 32768
NDEV = 128
FR = T // NDEV
CH = K // NDEV
RADIX = 4
KR = K // RADIX
GROUP = NDEV // RADIX
BLK = T // 128
PADBLK = 32
CHUNK = 8
STEPS = BLK // CHUNK
PARTS = 4
WIDE = 8
F32 = jnp.float32
BF16 = jnp.bfloat16
NT = (((1,), (1,)), ((), ()))
VMEM = pl.BlockSpec(memory_space=pltpu.VMEM)
SMEM = pl.BlockSpec(memory_space=pltpu.SMEM)
ANY = pl.BlockSpec(memory_space=pl.ANY)
MESH = pl.DeviceIdType.MESH


def hops(offset):
    return sum((0, 1, 2, 1)[offset[axis]] for axis in (0, 2, 3))


def offsets():
    mixed = [(n % 4, n // 64, (n // 4) % 4, (n // 16) % 4) for n in (i * 37 % NDEV for i in range(1, NDEV))]
    return sorted(mixed, key=lambda offset: -hops(offset))


def phase_of(offset):
    return 2 * (offset[0] % 2) + offset[1]


LAST_ORDER = offsets()
FIRST_ORDER = [offset for offset in LAST_ORDER if phase_of(offset) == 0]


def chan_tables():
    r = np.arange(RADIX)[:, None, None]
    i = np.arange(GROUP)[None, :, None]
    j = np.arange(CH)[None, None, :]
    chan = (NDEV * j + RADIX * i + r).reshape(-1)
    angle = (chan[:, None] * np.arange(KR)[None, :] % K) * (2.0 * math.pi / K)
    both = np.concatenate([np.cos(angle), np.sin(angle)], 1).astype(np.float32) * np.float32(1.0 / math.sqrt(K))
    return both.astype(ml_dtypes.bfloat16).reshape(RADIX, K // RADIX, 2 * KR)


def butterflies(held, taper, ya, yb, part):
    rows = FR // PARTS

    @pl.loop(0, rows // 16)
    def _(g):
        at = pl.ds(pl.multiple_of(part * rows + g * 16, 16), 16)
        for b in range(KR // 128):
            x = []
            for m in range(RADIX):
                lanes = pl.ds(m * KR + b * 128, 128)
                w = taper[:, lanes]
                x.append([(held[c, at, lanes] * w).astype(BF16).astype(F32) for c in range(2)])
            er, ei = x[0][0] + x[2][0], x[0][1] + x[2][1]
            fr, fi = x[1][0] + x[3][0], x[1][1] + x[3][1]
            gr, gi = x[0][0] - x[2][0], x[0][1] - x[2][1]
            hr, hi = x[1][0] - x[3][0], x[1][1] - x[3][1]
            y = [(er + fr, ei + fi), (gr + hi, gi - hr), (er - fr, ei - fi), (gr - hi, gi + hr)]
            for r in range(RADIX):
                re, im = y[r][0].astype(BF16), y[r][1].astype(BF16)
                ya[r, at, pl.ds(b * 128, 128)] = re
                ya[r, at, pl.ds(KR + b * 128, 128)] = im
                yb[r, at, pl.ds(b * 128, 128)] = im
                yb[r, at, pl.ds(KR + b * 128, 128)] = -re


def sincos(m, period):
    x = (m - period // 2).astype(F32) * (math.pi / period)
    z = x * x
    s = x * (1.0 + z * (-1.0 / 6 + z * (1.0 / 120 + z * (-1.0 / 5040 + z * (1.0 / 362880 - z / 39916800)))))
    c = 1.0 + z * (-0.5 + z * (1.0 / 24 + z * (-1.0 / 720 + z * (1.0 / 40320 + z * (-1.0 / 3628800 + z / 479001600)))))
    return 2.0 * s * s - 1.0, -2.0 * s * c


def rotated(e, f):
    return e[0] * f[0] - e[1] * f[1], e[0] * f[1] + e[1] * f[0]


def bins_of(bins, first, count):
    return jnp.concatenate([bins[pl.ds(first + i, 1), :] for i in range(count)], 1)


def frame_weights(bins, high, low, weight, beside):
    span = 8 * 128
    row32 = lax.broadcasted_iota(jnp.int32, (32, span), 0)

    @pl.loop(0, BLK // 8)
    def _(m):
        beside(m)
        b = bins_of(bins, m * 8, 8)
        lanes = pl.ds(pl.multiple_of(m * span, span), span)
        high[:, lanes] = ((b >> 5) == row32).astype(F32).astype(BF16)
        ones = ((b & 31) == row32).astype(F32).astype(BF16)
        low[0:32, lanes] = ones
        low[32:64, lanes] = ones

    part = 4096
    hist = jnp.zeros((32, 32), F32)
    for p in range(T // part):
        lanes = pl.ds(p * part, part)
        hist = hist + lax.dot_general(high[:, lanes], low[0:32, lanes], NT, preferred_element_type=F32)
    inverse = (1.0 / math.sqrt(NB)) / jnp.maximum(hist, 1.0)
    first = inverse.astype(BF16)
    second = (inverse - first.astype(F32)).astype(BF16)
    both = jnp.concatenate([first, second], 1)

    for p in range(T // part):
        lanes = pl.ds(p * part, part)
        rows = jnp.dot(both, low[:, lanes], preferred_element_type=F32)
        weight[:, lanes] = jnp.sum(rows * high[:, lanes].astype(F32), axis=0, keepdims=True)


def fill_table(bins, weight, table, beside):
    span = WIDE * 128
    odd = 2 * lax.broadcasted_iota(jnp.int32, (8, span), 0) + 1

    @pl.loop(0, BLK // WIDE)
    def _(m):
        beside(m)
        b = bins_of(bins, m * WIDE, WIDE)
        lanes = pl.ds(pl.multiple_of(m * span, span), span)
        w = weight[:, lanes]
        c, s = sincos((odd * b) & (NB - 1), NB)
        one = (c[0:1], s[0:1])
        even = rotated((c, s), one)
        turn = (even[0][7:8], even[1][7:8])
        twice = 2.0 * turn[0]
        for parity, start in ((0, (c, s)), (1, even)):
            before = (start[0] * w, start[1] * w)
            now = rotated(before, turn)
            for g in range(8):
                for k in range(2):
                    rows = pl.ds(k * NH + parity * 128 + g * 16, 16)
                    table[rows, lanes] = jnp.concatenate([before[k], now[k]], 0).astype(BF16)
                if g < 7:
                    after = (twice * now[0] - before[0], twice * now[1] - before[1])
                    later = (twice * after[0] - now[0], twice * after[1] - now[1])
                    before, now = after, later


def fill_mix(lags, mix):
    shape = (2 * CH, CH * 2 * L)
    row = lax.broadcasted_iota(jnp.int32, shape, 0)
    col = lax.broadcasted_iota(jnp.int32, shape, 1)
    part_in, chan_in = row >> 4, row & 15
    chan_out, part_out, q = col >> 4, (col >> 3) & 1, col & 7
    here = jnp.where(chan_in == chan_out, 1.0 / math.sqrt(L), 0.0)
    same = part_in == part_out
    sign = jnp.where(part_in == 0, -1.0, 1.0)
    for l in range(L):
        c, s = sincos((lags[l] * q) & (2 * MAXLAG - 1), 2 * MAXLAG)
        rows = pl.ds(l * 2 * CH, 2 * CH)
        mix[0, rows, :] = here * jnp.where(same, c, sign * s)
        mix[1, rows, :] = here * jnp.where(same, -s, sign * c)


def split_dot(a, b):
    a_high, b_high = a.astype(BF16), b.astype(BF16)
    a_low, b_low = (a - a_high.astype(F32)).astype(BF16), (b - b_high.astype(F32)).astype(BF16)
    small = jnp.dot(a_high, b_low, preferred_element_type=F32) + jnp.dot(a_low, b_high, preferred_element_type=F32)
    return jnp.dot(a_high, b_high, preferred_element_type=F32) + small


def spread_spectra(got, xs, first):
    @pl.loop(0, 4)
    def _(g):
        for e in range(4):
            s = first + g * 4 + e
            xs[2 * s] = got[s, :, 0:128]
            xs[2 * s + 1] = got[s, :, 128:256]


def fold(lags, xs, table, prod_a, prod_b, acc, step_at, count):
    lane = lax.broadcasted_iota(jnp.int32, (CH, 128), 1)

    def products(step, prod):
        first = step * CHUNK
        for l in range(L):
            lag = lags[l]
            whole, rest = lag >> 7, lag & 127
            back = (128 - rest) & 127
            inside = lane < 128 - rest
            moved = None
            for b in range(CHUNK + 1):
                there = xs[first + b + whole]
                ahead = [pltpu.roll(there[k * CH : (k + 1) * CH], back, 1) for k in range(2)]
                if b > 0:
                    here = xs[first + b - 1]
                    re, im = here[0:CH], here[CH : 2 * CH]
                    lre = jnp.where(inside, moved[0], ahead[0])
                    lim = jnp.where(inside, moved[1], ahead[1])
                    lanes = pl.ds((b - 1) * 128, 128)
                    prod[pl.ds(l * 2 * CH, CH), lanes] = re * lre + im * lim
                    prod[pl.ds(l * 2 * CH + CH, CH), lanes] = im * lre - re * lim
                moved = ahead

    def add(step, prod):
        lanes = pl.ds(pl.multiple_of(step * CHUNK * 128, CHUNK * 128), CHUNK * 128)
        acc[...] += lax.dot_general(prod[...], table[:, lanes], NT, preferred_element_type=F32)

    products(step_at(0), prod_a)

    @pl.loop(0, count // 2 - 1)
    def _(i):
        add(step_at(2 * i), prod_a)
        products(step_at(2 * i + 1), prod_b)
        add(step_at(2 * i + 1), prod_b)
        products(step_at(2 * i + 2), prod_a)

    add(step_at(count - 2), prod_a)
    products(step_at(count - 1), prod_b)
    add(step_at(count - 1), prod_b)


def kernel(
    lags, samples, taper, chans, own_bins, out,
    held, tab, ya, yb, spec, got, bins, weight, xs, table, prod_a, prod_b, acc, mix, mine, theirs,
    sem_s, sem_t, bin_send, bin_recv, spec_send, spec_recv, last_send, last_recv,
):
    tm, ch = lax.axis_index("tm"), lax.axis_index("chan")
    me = tm * 16 + ch
    x, core, z, y = tm // 2, tm % 2, ch // 4, ch % 4

    def partner(dx, dc, dz, dy):
        return ((x + dx) % 4) * 2 + (core + dc) % 2, ((z + dz) % 4) * 4 + (y + dy) % 4

    barrier = pltpu.get_barrier_semaphore()

    rows = FR // PARTS
    loads = []
    for p in range(PARTS):
        part = pl.ds(p * rows, rows)
        loads.append(pltpu.make_async_copy(samples.at[:, part], held.at[:, part], sem_s.at[p]))
        loads[-1].start()
    tables = []
    for r in range(RADIX):
        tables.append(pltpu.make_async_copy(chans.at[r], tab.at[r], sem_t.at[r]))
        tables[-1].start()

    for offset in LAST_ORDER:
        pl.semaphore_signal(barrier, inc=1, device_id=partner(*offset), device_id_type=MESH)

    for p in range(PARTS):
        loads[p].wait()
        butterflies(held, taper, ya, yb, p)

    for r in range(RADIX):
        tables[r].wait()
        re = lax.dot_general(tab[r], ya[r], NT, preferred_element_type=F32)
        spec[r, :, 0:CH, :] = re.astype(BF16).reshape(GROUP, CH, FR)
        im = lax.dot_general(tab[r], yb[r], NT, preferred_element_type=F32)
        spec[r, :, CH : 2 * CH, :] = im.astype(BF16).reshape(GROUP, CH, FR)

    pl.semaphore_wait(barrier, NDEV - 1)

    bins[pl.ds(pl.multiple_of(tm * 32, 32), 32), :] = own_bins[...]

    @pl.loop(1, 8)
    def _(i):
        pltpu.make_async_remote_copy(
            src_ref=own_bins,
            dst_ref=bins.at[pl.ds(pl.multiple_of(tm * 32, 32), 32)],
            send_sem=bin_send,
            recv_sem=bin_recv,
            device_id=((tm + i) % 8, ch),
            device_id_type=MESH,
        ).start()

    def send_spectra(offset, phase):
        to_tm, to_ch = partner(*offset)
        pltpu.make_async_remote_copy(
            src_ref=spec.at[(y + offset[3]) % 4, to_tm * 4 + to_ch // 4],
            dst_ref=got.at[me],
            send_sem=spec_send,
            recv_sem=spec_recv.at[phase],
            device_id=(to_tm, to_ch),
            device_id_type=MESH,
        ).start()

    for offset in FIRST_ORDER:
        send_spectra(offset, 0)

    got[me] = spec[y, tm * 4 + z]

    fill_mix(lags, mix)

    seven = pltpu.make_async_copy(bins.at[pl.ds(0, 224)], bins.at[pl.ds(0, 224)], bin_recv)
    seven.wait()
    high, low = table.at[pl.ds(0, 32)], table.at[pl.ds(32, 64)]
    def send_second(m):
        for k in range(2):
            late = m // 16
            n = ((2 * m + k) * 13) % 32
            send_spectra((late + 2 * (n % 2), 1 - late, (n // 2) % 4, n // 8), 1 + late)

    def send_last(m):
        n = (m * 13) % 32
        send_spectra((1 + 2 * (n % 2), 1, (n // 2) % 4, n // 8), 3)

    frame_weights(bins, high, low, weight, send_second)
    fill_table(bins, weight, table, send_last)

    acc[...] = jnp.zeros_like(acc)
    xs[pl.ds(BLK, PADBLK)] = jnp.zeros((PADBLK, 2 * CH, 128), BF16)

    def step_of(at_x, at_core, at_z):
        return (at_x % 4) * 8 + at_core * 4 + at_z

    def first_steps(i):
        return step_of(x + 2 * (i // 7), 0, i % 7)

    def inner(at_core):
        return lambda i: step_of(x + 1 + 2 * (i // 3), at_core, i % 3)

    def third_steps(i):
        late = i // 6
        return (1 - late) * inner(core)(i) + late * step_of(x + core + 2 * (i % 2), 1, 3)

    def fourth_steps(i):
        late, odd = i // 6, i // 8
        end = (1 - odd) * step_of(x + 1 + 2 * (i % 2), 0, 3) + odd * step_of(x + 1 - core + 2 * (i % 2), 1, 3)
        return (1 - late) * inner(1 - core)(i) + late * end

    for phase in range(4):
        shift, at_core = phase // 2, core if phase % 2 == 0 else 1 - core
        came = got.at[pl.ds(0, 31 if phase == 0 else 32)]
        pltpu.make_async_copy(came, came, spec_recv.at[phase]).wait()
        for k in range(2):
            spread_spectra(got, xs, ((x + shift + 2 * k) % 4) * 32 + at_core * 16)
        if phase > 0:
            step_at, count = ((first_steps, 14), (third_steps, 8), (fourth_steps, 10))[phase - 1]
            fold(lags, xs, table, prod_a, prod_b, acc, step_at, count)

    sums = acc[...].T
    res = split_dot(sums[0:NH], mix[0]) + split_dot(sums[NH:], mix[1])
    for p in range(2):
        for half in range(2):
            rows = res[p * 128 : (p + 1) * 128, half * 128 : (half + 1) * 128]
            mine[:, 2 * p + half, :] = rows

    for offset in LAST_ORDER:
        to_tm, to_ch = partner(*offset)
        pltpu.make_async_remote_copy(
            src_ref=mine.at[to_tm * 16 + to_ch],
            dst_ref=theirs.at[me],
            send_sem=last_send,
            recv_sem=last_recv,
            device_id=(to_tm, to_ch),
            device_id_type=MESH,
        ).start()
    theirs[me] = mine[me]
    rest = theirs.at[pl.ds(0, NDEV - 1)]
    pltpu.make_async_copy(rest, rest, last_recv).wait()

    for p in range(2):
        for half in range(2):
            turned = theirs[:, 2 * p + half, :].T
            for j in range(CH // 2):
                for ro in range(2):
                    row = j * 16 + ro * 8
                    lanes = pl.ds((half * (CH // 2) + j) * 128, 128)
                    out[ro, p, :, lanes] = turned[row : row + 8]

    sent = bins.at[pl.ds(0, 224)]
    pltpu.make_async_copy(sent, sent, bin_send).wait()
    blocks = got.at[pl.ds(0, NDEV - 1)]
    pltpu.make_async_copy(blocks, blocks, spec_send).wait()
    pltpu.make_async_copy(rest, rest, last_send).wait()


def on_device(samples, window_taper, phase_bins, lag_set):
    return pl.pallas_call(
        kernel,
        out_shape=jax.ShapeDtypeStruct((2, 2, L, K), F32),
        in_specs=[SMEM, ANY, VMEM, ANY, VMEM],
        out_specs=VMEM,
        scratch_shapes=[
            pltpu.VMEM((2, FR, K), F32),
            pltpu.VMEM((RADIX, K // RADIX, 2 * KR), BF16),
            pltpu.VMEM((RADIX, FR, 2 * KR), BF16),
            pltpu.VMEM((RADIX, FR, 2 * KR), BF16),
            pltpu.VMEM((RADIX, GROUP, 2 * CH, FR), BF16),
            pltpu.VMEM((NDEV, 2 * CH, FR), BF16),
            pltpu.VMEM((BLK, 128), jnp.int32),
            pltpu.VMEM((1, T), F32),
            pltpu.VMEM((BLK + PADBLK, 2 * CH, 128), BF16),
            pltpu.VMEM((2 * NH, T), BF16),
            pltpu.VMEM((L * 2 * CH, CHUNK * 128), BF16),
            pltpu.VMEM((L * 2 * CH, CHUNK * 128), BF16),
            pltpu.VMEM((L * 2 * CH, 2 * NH), F32),
            pltpu.VMEM((2, L * 2 * CH, CH * 2 * L), F32),
            pltpu.VMEM((NDEV, 4, 128), F32),
            pltpu.VMEM((NDEV, 4, 128), F32),
            pltpu.SemaphoreType.DMA((PARTS,)),
            pltpu.SemaphoreType.DMA((RADIX,)),
            pltpu.SemaphoreType.DMA,
            pltpu.SemaphoreType.DMA,
            pltpu.SemaphoreType.DMA,
            pltpu.SemaphoreType.DMA((4,)),
            pltpu.SemaphoreType.DMA,
            pltpu.SemaphoreType.DMA,
        ],
        compiler_params=pltpu.CompilerParams(
            vmem_limit_bytes=62 * 2**20, collective_id=0, has_side_effects=True
        ),
        name="cyclic",
    )(lag_set, samples, window_taper.reshape(1, K), jnp.asarray(chan_tables()), phase_bins.reshape(-1, 128))


def solution(mesh):
    placed = (P(None, ("tm", "chan"), None), P(), P("tm"), P())
    return jax.shard_map(
        on_device,
        mesh=mesh,
        in_specs=placed,
        out_specs=P(None, ("tm", "chan"), None, None),
        check_vma=False,
    )
```
